128 devices in a mesh: section: 2 (over y_hi), dp: 4 (over z), shard: 16 (over y_lo, x, core).
Axes of the slice: x: 4, y: 4 (y_hi: 2, y_lo: 2; y = y_hi * 2 + y_lo), z: 4, core: 2. Of those that a mesh axis runs over, the one named last changes fastest.
Arguments:
- ends: bfloat16 [2, 12288, 1024], P('section', ('dp', 'shard')), may hold values from -6 to 6
- segment_ids: int32 [12288], P(('dp', 'shard')), may hold values from 0 to 24, as said below
- token_mask: int32 [12288], P(('dp', 'shard')), may hold values from 0 to 1, as said below
- ln1_gain: bfloat16 [2, 1024], P('section', 'shard'), may hold values from 0.5 to 1.5
- ln1_bias: bfloat16 [2, 1024], P('section', 'shard'), may hold values from -2 to 2
- w_qkv: bfloat16 [2, 1024, 3072], P('section', 'shard'), may hold values from -0.1875 to 0.1875
- b_query: bfloat16 [2, 1024], P('section', 'shard'), may hold values from -3 to 3
- b_value: bfloat16 [2, 1024], P('section', 'shard'), may hold values from -3 to 3
- w_out: bfloat16 [2, 1024, 1024], P('section', 'shard'), may hold values from -0.75 to 0.75
- b_out: bfloat16 [2, 1024], P('section', 'shard'), may hold values from -3 to 3
- ln2_gain: bfloat16 [2, 1024], P('section', 'shard'), may hold values from 0.5 to 1.5
- ln2_bias: bfloat16 [2, 1024], P('section', 'shard'), may hold values from -2 to 2
- w_up: bfloat16 [2, 1024, 4096], P('section', 'shard'), may hold values from -0.1875 to 0.1875
- b_up: bfloat16 [2, 4096], P('section', 'shard'), may hold values from -3 to 3
- w_down: bfloat16 [2, 4096, 1024], P('section', 'shard'), may hold values from -0.1875 to 0.1875
- b_down: bfloat16 [2, 1024], P('section', 'shard'), may hold values from -3 to 3
Outputs:
- section_out: bfloat16 [2, 12288, 1024], P('section', ('dp', 'shard'))
- section_grad: bfloat16 [2, 12288, 1024], P('section', ('dp', 'shard'))
- grad_ln1_gain: float32 [2, 1024], P('section', 'shard')
- grad_ln1_bias: float32 [2, 1024], P('section', 'shard')
- grad_w_qkv: float32 [2, 1024, 3072], P('section', 'shard')
- grad_b_query: float32 [2, 1024], P('section', 'shard')
- grad_b_value: float32 [2, 1024], P('section', 'shard')
- grad_w_out: float32 [2, 1024, 1024], P('section', 'shard')
- grad_b_out: float32 [2, 1024], P('section', 'shard')
- grad_ln2_gain: float32 [2, 1024], P('section', 'shard')
- grad_ln2_bias: float32 [2, 1024], P('section', 'shard')
- grad_w_up: float32 [2, 1024, 4096], P('section', 'shard')
- grad_b_up: float32 [2, 4096], P('section', 'shard')
- grad_w_down: float32 [2, 4096, 1024], P('section', 'shard')
- grad_b_down: float32 [2, 1024], P('section', 'shard')
The draws below stay inside these ranges and needn't reach their ends.
Inputs may be any that keep to these rules, and one draw needn't show every extreme that they name: `segment_ids`: within each slot of 96 rows the ids start at 0 and never fall; a sequence never crosses a slot and starts at a row whose place in the slot is a multiple of 4; only the padding run that ends a slot may start elsewhere; the padding rows that end a slot share the id after the slot's last sequence. Groups along dp carry different amounts of padding, at most 48 rows a slot. `token_mask`: 1 on rows of sequences and 0 on the padding rows at the end of a slot.
All inputs are finite; a program needn't handle non-finite values.
Results may differ from the reference program's by a relative error of at most 0.025.
Values may be sent and summed in bfloat16 or wider, within the bound.
A program may use at most 384 MiB of HBM per device.

```python
import jax
import jax.numpy as jnp
from jax import lax

D = 1024
HEADS = 16
HEAD_DIM = 64
FF = 4096
SLOT = 96
GROUP_SLOTS = 32
TOKENS = 12288
N_SECTION = 2


def slot_layout(key):
    slot_count = TOKENS // SLOT
    break_key, pad_key = jax.random.split(jax.random.fold_in(key, 11))
    positions = jnp.arange(SLOT)[None, :]
    spread_limit = max(2, SLOT // 16)
    random_breaks = jax.random.randint(break_key, (slot_count, SLOT), 0, spread_limit) == 0
    first_slot = (jnp.arange(slot_count) == 0)[:, None]
    on_grid = positions % 4 == 0
    breaks = (random_breaks | first_slot) & on_grid
    group_index = jnp.arange(slot_count) // GROUP_SLOTS
    group_count = slot_count // GROUP_SLOTS
    pad_limit = 1 + (group_index + 1) * SLOT // (2 * group_count)
    padding = jax.random.randint(pad_key, (slot_count,), 0, pad_limit)
    padding = jnp.where(jnp.arange(slot_count) == 0, 1, padding)
    used_rows = (SLOT - padding)[:, None]
    starts = breaks & (positions > 0) & (positions < used_rows) | (positions == used_rows)
    segment = jnp.cumsum(starts.astype(jnp.int32), axis=1)
    live_rows = (positions < used_rows).astype(jnp.int32)
    return (segment.reshape(-1).astype(jnp.int32), live_rows.reshape(-1).astype(jnp.int32))


def draw_segment_ids(key, part):
    return slot_layout(key)[0]


def draw_token_mask(key, part):
    return slot_layout(key)[1]


def block_levels(key, shape, pieces, smallest, top_value):
    def one(axis_at, shards_of):
        steps = jax.random.uniform(jax.random.fold_in(jax.random.fold_in(key, 6), axis_at), (shards_of,), jnp.float32, smallest / len(pieces), top_value / len(pieces))
        return jnp.repeat(jnp.exp(steps), shape[axis_at] // shards_of).reshape((-1,) + (1,) * (len(shape) - axis_at - 1))

    gain = one(*pieces[0])
    for cut in pieces[1:]:
        gain = gain * one(*cut)
    return gain


def normal_values(key, dims, spread, bound, shards=(), held_as=jnp.bfloat16):
    drawn = spread * jax.random.normal(key, dims, jnp.float32)
    if shards:
        drawn = drawn * block_levels(key, dims, shards, -0.22, 0.18)
    return jnp.clip(drawn, -bound, bound).astype(held_as)


def setup_inputs(seed: int = 0) -> dict:
    arg_keys = jax.random.split(jax.random.key(seed), 17)
    ends = normal_values(arg_keys[0], (2, TOKENS, D), 1.0, 6.0, ((0, 2), (1, 64)))
    segment_ids = draw_segment_ids(jax.random.fold_in(arg_keys[16], 71), 0)
    token_mask = draw_token_mask(jax.random.fold_in(arg_keys[16], 71), 0)
    ln1_gain = jnp.clip(1.0 + 0.1 * jax.random.normal(arg_keys[3], (N_SECTION, D), jnp.float32), 0.5, 1.5).astype(jnp.bfloat16)
    ln1_bias = normal_values(arg_keys[4], (N_SECTION, D), 0.3, 2.0, ((0, 2), (1, 16)))
    w_qkv = normal_values(arg_keys[5], (N_SECTION, D, 3 * D), D ** -0.5, 0.1875, ((0, 2), (1, 16)))
    b_query = normal_values(arg_keys[6], (N_SECTION, D), 0.5, 3.0, ((0, 2), (1, 16)))
    b_value = normal_values(arg_keys[7], (N_SECTION, D), 0.5, 3.0, ((0, 2), (1, 16)))
    w_out = normal_values(arg_keys[8], (N_SECTION, D, D), (D // 16) ** -0.5, 0.75, ((0, 2), (1, 16)))
    b_out = normal_values(arg_keys[9], (N_SECTION, D), 0.5, 3.0, ((0, 2), (1, 16)))
    ln2_gain = jnp.clip(1.0 + 0.1 * jax.random.normal(arg_keys[10], (N_SECTION, D), jnp.float32), 0.5, 1.5).astype(jnp.bfloat16)
    ln2_bias = normal_values(arg_keys[11], (N_SECTION, D), 0.3, 2.0, ((0, 2), (1, 16)))
    w_up = normal_values(arg_keys[12], (N_SECTION, D, FF), D ** -0.5, 0.1875, ((0, 2), (1, 16)))
    b_up = normal_values(arg_keys[13], (N_SECTION, FF), 0.5, 3.0, ((0, 2), (1, 16)))
    w_down = normal_values(arg_keys[14], (N_SECTION, FF, D), (FF // 4) ** -0.5, 0.1875, ((0, 2), (1, 16)))
    b_down = normal_values(arg_keys[15], (N_SECTION, D), 0.5, 3.0, ((0, 2), (1, 16)))
    return {"ends": ends, "segment_ids": segment_ids, "token_mask": token_mask, "ln1_gain": ln1_gain, "ln1_bias": ln1_bias, "w_qkv": w_qkv, "b_query": b_query, "b_value": b_value, "w_out": w_out, "b_out": b_out, "ln2_gain": ln2_gain, "ln2_bias": ln2_bias, "w_up": w_up, "b_up": b_up, "w_down": w_down, "b_down": b_down}


@jax.custom_vjp
def low(v):
    return lax.optimization_barrier(v.astype(jnp.bfloat16)).astype(jnp.float32)

@jax.custom_vjp
def low_back(v):
    return v

def low_keep(v):
    return (low(v), None)

def low_pass(kept, grad):
    return (grad,)

def back_keep(v):
    return (v, None)

def back_low(kept, grad):
    return (low(grad),)
low.defvjp(low_keep, low_pass)
low_back.defvjp(back_keep, back_low)
norm_eps = 1e-05
masked_score = -1e+30

def matmul(left, right):
    return jnp.dot(left, right, precision=lax.Precision.HIGHEST, preferred_element_type=jnp.float32)

def normalize(values, norm_gain, norm_bias):
    row_mean = lax.optimization_barrier(jnp.mean(values, axis=-1, keepdims=True))
    centered = values - row_mean
    variance = lax.optimization_barrier(jnp.mean(centered * centered, axis=-1, keepdims=True))
    return centered * lax.rsqrt(variance + norm_eps) * norm_gain + norm_bias

def attend_slot(queries, keys_part, values_part, segment):
    positions = jnp.arange(SLOT)
    allowed = (segment[:, None] == segment[None, :]) & (positions[None, :] <= positions[:, None])
    query_heads = queries.reshape(SLOT, HEADS, HEAD_DIM)
    key_heads = keys_part.reshape(SLOT, HEADS, HEAD_DIM)
    value_heads = values_part.reshape(SLOT, HEADS, HEAD_DIM)
    score_scale = HEAD_DIM ** (-0.5)
    scores = jnp.einsum('qhd,khd->hqk', query_heads, key_heads, precision=lax.Precision.HIGHEST) * score_scale
    scores = low_back(scores)
    attn_probs = jax.nn.softmax(jnp.where(allowed[None], scores, masked_score), axis=-1)
    attn_probs = low(attn_probs)
    attended = jnp.einsum('hqk,khd->qhd', attn_probs, value_heads, precision=lax.Precision.HIGHEST)
    return attended.reshape(SLOT, D)

def layer(inputs, params, segment):
    gain_one, bias_one, w_joint, bias_query, bias_value, w_mix, bias_mix, gain_two, bias_two, w_grow, bias_grow, w_shrink, bias_shrink = params
    normed = low(normalize(inputs, gain_one, bias_one))
    projected = matmul(normed, w_joint)
    queries = low_back(low(projected[:, :D] + bias_query))
    keys_part = low_back(low(projected[:, D:2 * D]))
    values_part = low_back(low(projected[:, 2 * D:] + bias_value))
    slot_count = inputs.shape[0] // SLOT
    members = (queries.reshape(slot_count, SLOT, D), keys_part.reshape(slot_count, SLOT, D), values_part.reshape(slot_count, SLOT, D), segment.reshape(slot_count, SLOT))
    attended = lax.map(jax.checkpoint(lambda item_set: attend_slot(*item_set)), members)
    attended = low_back(low(attended.reshape(inputs.shape[0], D)))
    branch = low_back(matmul(attended, w_mix) + bias_mix)
    middle = inputs + branch
    second = low(normalize(middle, gain_two, bias_two))
    before = low_back(matmul(second, w_grow) + bias_grow)
    hidden = low(jax.nn.gelu(before, approximate=True))
    update = low_back(matmul(hidden, w_shrink) + bias_shrink)
    return middle + update

def reference(ends, segment_ids, token_mask, ln1_gain, ln1_bias, w_qkv, b_query, b_value, w_out, b_out, ln2_gain, ln2_bias, w_up, b_up, w_down, b_down):
    stacked = (ln1_gain, ln1_bias, w_qkv, b_query, b_value, w_out, b_out, ln2_gain, ln2_bias, w_up, b_up, w_down, b_down)
    first_layer = tuple((v[0].astype(jnp.float32) for v in stacked))
    last_layer = tuple((v[1].astype(jnp.float32) for v in stacked))
    group_rows = GROUP_SLOTS * SLOT
    group_count = TOKENS // group_rows
    inputs = ends[0].astype(jnp.float32).reshape(group_count, group_rows, D)
    cotangent = (ends[1].astype(jnp.float32) * token_mask.astype(jnp.float32)[:, None]).reshape(group_count, group_rows, D)
    segments = segment_ids.reshape(group_count, group_rows)

    def one_group(carry, members):
        block_in, block_cot, block_seg = members
        first_out, first_pull = jax.vjp(lambda a, b: layer(a, b, block_seg), block_in, first_layer)
        sent = low(first_out)
        last_out, last_pull = jax.vjp(lambda a, b: layer(a, b, block_seg), sent, last_layer)
        grad_sent, grad_last = last_pull(block_cot)
        sent_grad = low(grad_sent)
        grad_input, grad_first = first_pull(sent_grad)
        carry = (jax.tree.map(jnp.add, carry[0], grad_first), jax.tree.map(jnp.add, carry[1], grad_last))
        return (carry, (first_out.astype(jnp.bfloat16), last_out.astype(jnp.bfloat16), grad_input.astype(jnp.bfloat16), sent_grad.astype(jnp.bfloat16)))
    start_carry = jax.tree.map(jnp.zeros_like, (first_layer, last_layer))
    (sum_first, sum_last), produced = lax.scan(one_group, start_carry, (inputs, cotangent, segments))
    first_out, last_out, grad_input, sent_grad = produced
    section_out = jnp.stack([first_out.reshape(TOKENS, D), last_out.reshape(TOKENS, D)])
    section_grad = jnp.stack([grad_input.reshape(TOKENS, D), sent_grad.reshape(TOKENS, D)])
    grads = [jnp.stack([a, b]) for a, b in zip(sum_first, sum_last)]
    return (section_out, section_grad, grads[0], grads[1], grads[2], grads[3], grads[4], grads[5], grads[6], grads[7], grads[8], grads[9], grads[10], grads[11], grads[12])
```

```python
import functools

import jax
import jax.numpy as jnp
from jax import lax
from jax.sharding import PartitionSpec as P

HEADS = 16
SLOT = 96

norm_eps = 1e-05
masked_score = -1e30


def swap_section(value, steps):
    pairs = [(0, 1)] if steps > 0 else [(1, 0)]
    return lax.ppermute(value, "section", pairs)


def normalize(values, norm_gain, norm_bias):
    row_mean = jnp.mean(values, axis=-1, keepdims=True)
    centered = values - row_mean
    variance = jnp.mean(centered * centered, axis=-1, keepdims=True)
    return centered * lax.rsqrt(variance + norm_eps) * norm_gain + norm_bias


def dot(left, right):
    return jnp.dot(left, right, preferred_element_type=jnp.float32)


def dot_rows(left, right):
    return lax.dot_general(
        left, right, (((0,), (0,)), ((), ())), preferred_element_type=jnp.float32
    )


def dot_back(left, right):
    return lax.dot_general(
        left, right, (((1,), (1,)), ((), ())), preferred_element_type=jnp.float32
    )


def split_heads(values):
    return values.reshape(values.shape[0], HEADS, values.shape[1] // HEADS)


def allowed_pairs(segment):
    positions = jnp.arange(segment.shape[0])
    slot_of = positions // SLOT
    return (
        (segment[:, None] == segment[None, :])
        & (positions[None, :] <= positions[:, None])
        & (slot_of[:, None] == slot_of[None, :])
    )


def head_scores(queries, keys_part, allowed):
    score_scale = (queries.shape[1] // HEADS) ** (-0.5)
    raw_scores = (
        jnp.einsum(
            "qhd,khd->hqk",
            split_heads(queries),
            split_heads(keys_part),
            preferred_element_type=jnp.float32,
        )
        * score_scale
    )
    return jnp.where(allowed[None], raw_scores, masked_score)


def forward(rows_in, allowed, mats, vecs):
    w_qkv, w_out, w_up, w_down = mats
    width = rows_in.shape[1]
    inputs = rows_in.astype(jnp.float32)
    normed = normalize(inputs, vecs["ln1_gain"], vecs["ln1_bias"]).astype(jnp.bfloat16)
    projected = dot(normed, w_qkv)
    queries = (projected[:, :width] + vecs["b_query"]).astype(jnp.bfloat16)
    keys_part = projected[:, width : 2 * width].astype(jnp.bfloat16)
    values_part = (projected[:, 2 * width :] + vecs["b_value"]).astype(jnp.bfloat16)
    scores = head_scores(queries, keys_part, allowed)
    row_top = jnp.max(scores, axis=-1, keepdims=True)
    exponent = jnp.exp(scores - row_top)
    row_total = jnp.sum(exponent, axis=-1, keepdims=True)
    attn_probs = exponent / row_total
    row_lse = row_top + jnp.log(row_total)
    attended = (
        jnp.einsum(
            "hqk,khd->qhd",
            attn_probs.astype(jnp.bfloat16),
            split_heads(values_part),
            preferred_element_type=jnp.float32,
        )
        .reshape(rows_in.shape)
        .astype(jnp.bfloat16)
    )
    middle = inputs + dot(attended, w_out) + vecs["b_out"]
    second = normalize(middle, vecs["ln2_gain"], vecs["ln2_bias"]).astype(jnp.bfloat16)
    before = dot(second, w_up) + vecs["b_up"]
    hidden = jax.nn.gelu(before, approximate=True).astype(jnp.bfloat16)
    result = middle + dot(hidden, w_down) + vecs["b_down"]
    record = (inputs, normed, queries, keys_part, values_part, row_lse, attended, middle, second, before, hidden)
    return result.astype(jnp.bfloat16), record


def backward_rows(grad_out, record, allowed, mats, vecs):
    w_qkv, w_out, w_up, w_down = mats
    inputs, normed, queries, keys_part, values_part, row_lse, attended, middle, second, before, hidden = record
    width = inputs.shape[1]
    grad_update = grad_out.astype(jnp.bfloat16)
    grad_hidden = dot_back(grad_update, w_down)
    _, gelu_pull = jax.vjp(functools.partial(jax.nn.gelu, approximate=True), before)
    grad_before = gelu_pull(grad_hidden)[0].astype(jnp.bfloat16)
    grad_second = dot_back(grad_before, w_up)
    _, second_pull = jax.vjp(normalize, middle, vecs["ln2_gain"], vecs["ln2_bias"])
    grad_mid_norm, grad_gain_two, grad_bias_two = second_pull(grad_second)
    grad_middle = grad_out + grad_mid_norm
    grad_branch = grad_middle.astype(jnp.bfloat16)
    grad_attended = dot_back(grad_branch, w_out).astype(jnp.bfloat16)
    score_scale = (width // HEADS) ** (-0.5)
    attn_probs = jnp.exp(head_scores(queries, keys_part, allowed) - row_lse)
    grad_heads = split_heads(grad_attended)
    grad_probs = jnp.einsum(
        "qhd,khd->hqk", grad_heads, split_heads(values_part), preferred_element_type=jnp.float32
    )
    row_delta = jnp.sum(attn_probs * grad_probs, axis=-1, keepdims=True)
    grad_scores = (attn_probs * (grad_probs - row_delta)).astype(jnp.bfloat16)
    grad_query = (
        jnp.einsum("hqk,khd->qhd", grad_scores, split_heads(keys_part), preferred_element_type=jnp.float32)
        * score_scale
    )
    grad_key = (
        jnp.einsum("hqk,qhd->khd", grad_scores, split_heads(queries), preferred_element_type=jnp.float32)
        * score_scale
    )
    grad_value = jnp.einsum(
        "hqk,qhd->khd", attn_probs.astype(jnp.bfloat16), grad_heads, preferred_element_type=jnp.float32
    )
    grad_joined = jnp.concatenate(
        [v.reshape(inputs.shape) for v in (grad_query, grad_key, grad_value)], axis=1
    ).astype(jnp.bfloat16)
    _, first_pull = jax.vjp(normalize, inputs, vecs["ln1_gain"], vecs["ln1_bias"])
    grad_normed = dot_back(grad_joined, w_qkv)
    grad_in_norm, grad_gain_one, grad_bias_one = first_pull(grad_normed)
    grad_in = (grad_middle + grad_in_norm).astype(jnp.bfloat16)
    sides = (grad_update, grad_before, grad_branch, grad_joined)
    norm_sums = (grad_gain_one, grad_bias_one, grad_gain_two, grad_bias_two)
    return grad_in, sides, norm_sums


def column_sum(values):
    return jnp.sum(values.astype(jnp.float32), axis=0)


def on_device(
    ends, segment_ids, token_mask,
    ln1_gain, ln1_bias, w_qkv, b_query, b_value, w_out, b_out,
    ln2_gain, ln2_bias, w_up, b_up, w_down, b_down,
):
    names = ("ln1_gain", "ln1_bias", "b_query", "b_value", "b_out", "ln2_gain", "ln2_bias", "b_down", "b_up")
    shards = (ln1_gain, ln1_bias, b_query, b_value, b_out, ln2_gain, ln2_bias, b_down, b_up)
    packed = jnp.concatenate([v[0] for v in shards])
    everyone = lax.all_gather(packed, "shard", axis=0, tiled=False).astype(jnp.float32)
    vecs, at = {}, 0
    for name, v in zip(names, shards):
        vecs[name] = everyone[:, at : at + v.shape[1]].reshape(1, -1)
        at += v.shape[1]
    mats = tuple(lax.all_gather(w[0], "shard", axis=0, tiled=True) for w in (w_qkv, w_out, w_up, w_down))

    first_section = lax.axis_index("section") == 0
    local_rows = ends[0]
    allowed = allowed_pairs(segment_ids)

    early, _ = forward(local_rows, allowed, mats, vecs)
    arrived = swap_section(early, 1)
    own_rows = jnp.where(first_section, local_rows, arrived)
    section_out, record = forward(own_rows, allowed, mats, vecs)

    cotangent = local_rows.astype(jnp.float32) * token_mask[:, None].astype(jnp.float32)
    early_grad, _, _ = backward_rows(cotangent, record, allowed, mats, vecs)
    came_back = swap_section(early_grad, -1)
    grad_now = jnp.where(first_section, came_back.astype(jnp.float32), cotangent)
    section_grad, sides, norm_sums = backward_rows(grad_now, record, allowed, mats, vecs)

    grad_update, grad_before, grad_branch, grad_joined = sides
    inputs, normed, _, _, _, _, attended, _, second, _, hidden = record
    width = inputs.shape[1]
    partial = [
        dot_rows(left, right).astype(jnp.bfloat16)
        for left, right in (
            (hidden, grad_update), (second, grad_before), (attended, grad_branch), (normed, grad_joined)
        )
    ]
    summed = [lax.psum_scatter(p, "shard", scatter_dimension=0, tiled=True) for p in partial]
    summed = [lax.psum(s, "dp").astype(jnp.float32)[None] for s in summed]
    g_down, g_up, g_out, g_qkv = summed
    gain_one, bias_one, gain_two, bias_two = norm_sums
    vectors = [
        gain_one, bias_one, column_sum(grad_joined[:, :width])[None], column_sum(grad_joined[:, 2 * width :])[None],
        column_sum(grad_branch)[None], gain_two, bias_two, column_sum(grad_update)[None],
        column_sum(grad_before)[None],
    ]
    shard_count = lax.axis_size("shard")
    rows = jnp.concatenate([v.reshape(shard_count, -1) for v in vectors], axis=1)
    rows = lax.psum(rows, ("shard", "dp"))
    mine = lax.dynamic_slice_in_dim(rows, lax.axis_index("shard"), 1, 0)
    out, at = {}, 0
    for name, v in zip(names, shards):
        out[name] = mine[:, at : at + v.shape[1]]
        at += v.shape[1]
    return (
        section_out[None], section_grad[None], out["ln1_gain"], out["ln1_bias"], g_qkv, out["b_query"],
        out["b_value"], g_out, out["b_out"], out["ln2_gain"], out["ln2_bias"], g_up, out["b_up"], g_down,
        out["b_down"],
    )


def solution(mesh):
    vector, matrix = P("section", "shard"), P("section", "shard", None)
    rows, ids = P("section", ("dp", "shard"), None), P(("dp", "shard"))
    in_specs = (
        rows, ids, ids, vector, vector, matrix, vector, vector, matrix, vector, vector, vector, matrix,
        vector, matrix, vector,
    )
    out_specs = (
        rows, rows, vector, vector, matrix, vector, vector, matrix, vector, vector, vector, matrix, vector,
        matrix, vector,
    )
    return jax.shard_map(on_device, mesh=mesh, in_specs=in_specs, out_specs=out_specs, check_vma=False)
```

```python
import functools

import jax
import jax.numpy as jnp
from jax import lax
from jax.experimental import pallas as pl
from jax.experimental.pallas import tpu as pltpu
from jax.sharding import PartitionSpec as P

HEADS = 16
SLOT = 96

norm_eps = 1e-05
masked_score = -1e30
MESH = pl.DeviceIdType.MESH
RING_FIRST = (1, 3)


def gather_kernel(count, *refs):
    shards, fulls = refs[:count], refs[count : 2 * count]
    own_sem, send_sem, recv_sem = refs[2 * count :]
    me = lax.axis_index("shard")
    core, x, y = me % 2, (me // 2) % 4, me // 8

    def at(dy, dx):
        return (((y + dy) % 2) * 4 + (x + dx) % 4) * 2 + core

    sibling = me + 1 - 2 * core
    right, left, pair = at(0, 1), at(0, 3), at(1, 0)
    barrier = pltpu.get_barrier_semaphore()
    for other in (sibling, right, left, pair):
        pl.semaphore_signal(barrier, inc=1, device_id={"shard": other}, device_id_type=MESH)
    pl.semaphore_wait(barrier, 4)

    began = []

    def send(which, dy, dx, target, half=None):
        rows, width = shards[which].shape
        mine = dy == 0 and dx == 0
        spot = pl.ds(pl.multiple_of(at(dy, dx) * rows, 16), rows)
        cut = pl.ds(0, width) if half is None else pl.ds(half * (width // 2), width // 2)
        source = shards[which].at[:, cut] if mine else fulls[which].at[spot, cut]
        copy = pltpu.make_async_remote_copy(
            src_ref=source,
            dst_ref=fulls[which].at[spot, cut],
            send_sem=send_sem.at[len(began)],
            recv_sem=recv_sem.at[len(began)],
            device_id={"shard": target},
            device_id_type=MESH,
        )
        copy.start()
        began.append(copy)
        return copy

    pair_first = [k for k in range(count) if k not in RING_FIRST]
    ring_first = [k for k in range(count) if k in RING_FIRST]
    kept = []
    for k in range(count):
        rows = shards[k].shape[0]
        spot = pl.ds(pl.multiple_of(me * rows, 16), rows)
        copy = pltpu.make_async_copy(shards[k], fulls[k].at[spot, :], own_sem.at[k])
        copy.start()
        kept.append(copy)
    to_pair, to_right, to_left, shared = {}, {}, {}, []
    for k in pair_first:
        to_pair[k] = send(k, 0, 0, pair)
    for k in ring_first + pair_first:
        to_right[k] = send(k, 0, 0, right)
        to_left[k] = send(k, 0, 0, left)
    for k in ring_first:
        to_pair[k] = send(k, 0, 0, pair)
    for k in range(count):
        shared.append(send(k, 0, 0, sibling))
    pair_right, pair_left = {}, {}
    for k in pair_first:
        to_pair[k].wait_recv()
        pair_right[k] = send(k, 1, 0, right)
        pair_left[k] = send(k, 1, 0, left)
        shared.append(send(k, 1, 0, sibling))
    far, ring_pair = {}, {}
    for k in ring_first + pair_first:
        to_right[k].wait_recv()
        far[k, 0] = send(k, 0, 3, right, 0)
        if k in ring_first:
            ring_pair[k, 3] = send(k, 0, 3, pair)
        shared.append(send(k, 0, 3, sibling))
        to_left[k].wait_recv()
        far[k, 1] = send(k, 0, 1, left, 1)
        if k in ring_first:
            ring_pair[k, 1] = send(k, 0, 1, pair)
        shared.append(send(k, 0, 1, sibling))
    for k in ring_first:
        to_pair[k].wait_recv()
        shared.append(send(k, 1, 0, sibling))
    for k in ring_first:
        far[k, 0].wait_recv()
        far[k, 1].wait_recv()
        ring_pair[k, 2] = send(k, 0, 2, pair)
        shared.append(send(k, 0, 2, sibling))
    far_pair = {}
    for k in pair_first:
        pair_right[k].wait_recv()
        far_pair[k, 0] = send(k, 1, 3, right, 0)
        shared.append(send(k, 1, 3, sibling))
        pair_left[k].wait_recv()
        far_pair[k, 1] = send(k, 1, 1, left, 1)
        shared.append(send(k, 1, 1, sibling))
    for k in pair_first:
        far[k, 0].wait_recv()
        far[k, 1].wait_recv()
        shared.append(send(k, 0, 2, sibling))
    for k in ring_first:
        for dx in (3, 1):
            ring_pair[k, dx].wait_recv()
            shared.append(send(k, 1, dx, sibling))
    for k in pair_first:
        far_pair[k, 0].wait_recv()
        far_pair[k, 1].wait_recv()
        shared.append(send(k, 1, 2, sibling))
    for k in ring_first:
        ring_pair[k, 2].wait_recv()
        shared.append(send(k, 1, 2, sibling))
    for copy in shared:
        copy.wait_recv()
    for copy in began:
        copy.wait_send()
    for copy in kept:
        copy.wait()


def gather_all(arrays):
    count = len(arrays)
    copies = sum(16 if k in RING_FIRST else 17 for k in range(count))
    return pl.pallas_call(
        functools.partial(gather_kernel, count),
        out_shape=[jax.ShapeDtypeStruct((16 * a.shape[0], a.shape[1]), a.dtype) for a in arrays],
        in_specs=[pl.BlockSpec(memory_space=pl.ANY)] * count,
        out_specs=[pl.BlockSpec(memory_space=pl.ANY)] * count,
        scratch_shapes=[
            pltpu.SemaphoreType.DMA((count,)),
            pltpu.SemaphoreType.DMA((copies,)),
            pltpu.SemaphoreType.DMA((copies,)),
        ],
        compiler_params=pltpu.CompilerParams(collective_id=0, has_side_effects=True),
    )(*arrays)


def swap_section(value, steps):
    pairs = [(0, 1)] if steps > 0 else [(1, 0)]
    return lax.ppermute(value, "section", pairs)


def normalize(values, norm_gain, norm_bias):
    row_mean = jnp.mean(values, axis=-1, keepdims=True)
    centered = values - row_mean
    variance = jnp.mean(centered * centered, axis=-1, keepdims=True)
    return centered * lax.rsqrt(variance + norm_eps) * norm_gain + norm_bias


def dot(left, right):
    return jnp.dot(left, right, preferred_element_type=jnp.float32)


def dot_rows(left, right):
    return lax.dot_general(
        left, right, (((0,), (0,)), ((), ())), preferred_element_type=jnp.float32
    )


def dot_back(left, right):
    return lax.dot_general(
        left, right, (((1,), (1,)), ((), ())), preferred_element_type=jnp.float32
    )


def split_heads(values):
    return values.reshape(values.shape[0], HEADS, values.shape[1] // HEADS)


def allowed_pairs(segment):
    positions = jnp.arange(segment.shape[0])
    slot_of = positions // SLOT
    return (
        (segment[:, None] == segment[None, :])
        & (positions[None, :] <= positions[:, None])
        & (slot_of[:, None] == slot_of[None, :])
    )


def head_scores(queries, keys_part, allowed):
    score_scale = (queries.shape[1] // HEADS) ** (-0.5)
    raw_scores = (
        jnp.einsum(
            "qhd,khd->hqk",
            split_heads(queries),
            split_heads(keys_part),
            preferred_element_type=jnp.float32,
        )
        * score_scale
    )
    return jnp.where(allowed[None], raw_scores, masked_score)


def forward(rows_in, allowed, mats, vecs):
    w_qkv, w_out, w_up, w_down = mats
    width = rows_in.shape[1]
    inputs = rows_in.astype(jnp.float32)
    normed = normalize(inputs, vecs["ln1_gain"], vecs["ln1_bias"]).astype(jnp.bfloat16)
    projected = dot(normed, w_qkv)
    queries = (projected[:, :width] + vecs["b_query"]).astype(jnp.bfloat16)
    keys_part = projected[:, width : 2 * width].astype(jnp.bfloat16)
    values_part = (projected[:, 2 * width :] + vecs["b_value"]).astype(jnp.bfloat16)
    scores = head_scores(queries, keys_part, allowed)
    row_top = jnp.max(scores, axis=-1, keepdims=True)
    exponent = jnp.exp(scores - row_top)
    row_total = jnp.sum(exponent, axis=-1, keepdims=True)
    attn_probs = exponent / row_total
    row_lse = row_top + jnp.log(row_total)
    attended = (
        jnp.einsum(
            "hqk,khd->qhd",
            attn_probs.astype(jnp.bfloat16),
            split_heads(values_part),
            preferred_element_type=jnp.float32,
        )
        .reshape(rows_in.shape)
        .astype(jnp.bfloat16)
    )
    middle = inputs + dot(attended, w_out) + vecs["b_out"]
    second = normalize(middle, vecs["ln2_gain"], vecs["ln2_bias"]).astype(jnp.bfloat16)
    before = dot(second, w_up) + vecs["b_up"]
    hidden = jax.nn.gelu(before, approximate=True).astype(jnp.bfloat16)
    result = middle + dot(hidden, w_down) + vecs["b_down"]
    record = (inputs, normed, queries, keys_part, values_part, row_lse, attended, middle, second, before, hidden)
    return result.astype(jnp.bfloat16), record


def backward_rows(grad_out, record, allowed, mats, vecs):
    w_qkv, w_out, w_up, w_down = mats
    inputs, normed, queries, keys_part, values_part, row_lse, attended, middle, second, before, hidden = record
    width = inputs.shape[1]
    grad_update = grad_out.astype(jnp.bfloat16)
    grad_hidden = dot_back(grad_update, w_down)
    _, gelu_pull = jax.vjp(functools.partial(jax.nn.gelu, approximate=True), before)
    grad_before = gelu_pull(grad_hidden)[0].astype(jnp.bfloat16)
    grad_second = dot_back(grad_before, w_up)
    _, second_pull = jax.vjp(normalize, middle, vecs["ln2_gain"], vecs["ln2_bias"])
    grad_mid_norm, grad_gain_two, grad_bias_two = second_pull(grad_second)
    grad_middle = grad_out + grad_mid_norm
    grad_branch = grad_middle.astype(jnp.bfloat16)
    grad_attended = dot_back(grad_branch, w_out).astype(jnp.bfloat16)
    score_scale = (width // HEADS) ** (-0.5)
    attn_probs = jnp.exp(head_scores(queries, keys_part, allowed) - row_lse)
    grad_heads = split_heads(grad_attended)
    grad_probs = jnp.einsum(
        "qhd,khd->hqk", grad_heads, split_heads(values_part), preferred_element_type=jnp.float32
    )
    row_delta = jnp.sum(attn_probs * grad_probs, axis=-1, keepdims=True)
    grad_scores = (attn_probs * (grad_probs - row_delta)).astype(jnp.bfloat16)
    grad_query = (
        jnp.einsum("hqk,khd->qhd", grad_scores, split_heads(keys_part), preferred_element_type=jnp.float32)
        * score_scale
    )
    grad_key = (
        jnp.einsum("hqk,qhd->khd", grad_scores, split_heads(queries), preferred_element_type=jnp.float32)
        * score_scale
    )
    grad_value = jnp.einsum(
        "hqk,qhd->khd", attn_probs.astype(jnp.bfloat16), grad_heads, preferred_element_type=jnp.float32
    )
    grad_joined = jnp.concatenate(
        [v.reshape(inputs.shape) for v in (grad_query, grad_key, grad_value)], axis=1
    ).astype(jnp.bfloat16)
    _, first_pull = jax.vjp(normalize, inputs, vecs["ln1_gain"], vecs["ln1_bias"])
    grad_normed = dot_back(grad_joined, w_qkv)
    grad_in_norm, grad_gain_one, grad_bias_one = first_pull(grad_normed)
    grad_in = (grad_middle + grad_in_norm).astype(jnp.bfloat16)
    sides = (grad_update, grad_before, grad_branch, grad_joined)
    norm_sums = (grad_gain_one, grad_bias_one, grad_gain_two, grad_bias_two)
    return grad_in, sides, norm_sums


def column_sum(values):
    return jnp.sum(values.astype(jnp.float32), axis=0)


def on_device(
    ends, segment_ids, token_mask,
    ln1_gain, ln1_bias, w_qkv, b_query, b_value, w_out, b_out,
    ln2_gain, ln2_bias, w_up, b_up, w_down, b_down,
):
    names = ("ln1_gain", "ln1_bias", "b_query", "b_value", "b_out", "ln2_gain", "ln2_bias", "b_down", "b_up")
    shards = (ln1_gain, ln1_bias, b_query, b_value, b_out, ln2_gain, ln2_bias, b_down, b_up)
    packed = jnp.concatenate([v[0] for v in shards])
    tall = jnp.broadcast_to(packed[None], (16, packed.shape[0]))
    *mats, everyone = gather_all((w_qkv[0], w_out[0], w_up[0], w_down[0], tall))
    everyone = everyone.reshape(-1, *tall.shape)[:, 0].astype(jnp.float32)
    vecs, at = {}, 0
    for name, v in zip(names, shards):
        vecs[name] = everyone[:, at : at + v.shape[1]].reshape(1, -1)
        at += v.shape[1]

    first_section = lax.axis_index("section") == 0
    local_rows = ends[0]
    allowed = allowed_pairs(segment_ids)

    early, _ = forward(local_rows, allowed, mats, vecs)
    arrived = swap_section(early, 1)
    own_rows = jnp.where(first_section, local_rows, arrived)
    section_out, record = forward(own_rows, allowed, mats, vecs)

    cotangent = local_rows.astype(jnp.float32) * token_mask[:, None].astype(jnp.float32)
    early_grad, _, _ = backward_rows(cotangent, record, allowed, mats, vecs)
    came_back = swap_section(early_grad, -1)
    grad_now = jnp.where(first_section, came_back.astype(jnp.float32), cotangent)
    section_grad, sides, norm_sums = backward_rows(grad_now, record, allowed, mats, vecs)

    grad_update, grad_before, grad_branch, grad_joined = sides
    inputs, normed, _, _, _, _, attended, _, second, _, hidden = record
    width = inputs.shape[1]
    partial = [
        dot_rows(left, right).astype(jnp.bfloat16)
        for left, right in (
            (hidden, grad_update), (second, grad_before), (attended, grad_branch), (normed, grad_joined)
        )
    ]
    summed = [lax.psum_scatter(p, "shard", scatter_dimension=0, tiled=True) for p in partial]
    summed = [lax.psum(s, "dp").astype(jnp.float32)[None] for s in summed]
    g_down, g_up, g_out, g_qkv = summed
    gain_one, bias_one, gain_two, bias_two = norm_sums
    vectors = [
        gain_one, bias_one, column_sum(grad_joined[:, :width])[None], column_sum(grad_joined[:, 2 * width :])[None],
        column_sum(grad_branch)[None], gain_two, bias_two, column_sum(grad_update)[None],
        column_sum(grad_before)[None],
    ]
    shard_count = lax.axis_size("shard")
    rows = jnp.concatenate([v.reshape(shard_count, -1) for v in vectors], axis=1)
    rows = lax.psum(lax.psum(rows, "shard"), "dp")
    mine = lax.dynamic_slice_in_dim(rows, lax.axis_index("shard"), 1, 0)
    out, at = {}, 0
    for name, v in zip(names, shards):
        out[name] = mine[:, at : at + v.shape[1]]
        at += v.shape[1]
    return (
        section_out[None], section_grad[None], out["ln1_gain"], out["ln1_bias"], g_qkv, out["b_query"],
        out["b_value"], g_out, out["b_out"], out["ln2_gain"], out["ln2_bias"], g_up, out["b_up"], g_down,
        out["b_down"],
    )


def solution(mesh):
    vector, matrix = P("section", "shard"), P("section", "shard", None)
    rows, ids = P("section", ("dp", "shard"), None), P(("dp", "shard"))
    in_specs = (
        rows, ids, ids, vector, vector, matrix, vector, vector, matrix, vector, vector, vector, matrix,
        vector, matrix, vector,
    )
    out_specs = (
        rows, rows, vector, vector, matrix, vector, vector, matrix, vector, vector, vector, matrix, vector,
        matrix, vector,
    )
    return jax.shard_map(on_device, mesh=mesh, in_specs=in_specs, out_specs=out_specs, check_vma=False)
```

```python
import collections
import functools
import math

import jax
import jax.numpy as jnp
from jax import lax
from jax.experimental import pallas as pl
from jax.experimental.pallas import tpu as pltpu
from jax.sharding import PartitionSpec as P

HEADS = 16
SLOT = 96
GELU_A = math.sqrt(2.0 / math.pi)
GELU_B = 0.044715

norm_eps = 1e-05
masked_score = -1e30
MESH = pl.DeviceIdType.MESH
RING_FIRST = (1, 3)


def dot(left, right):
    return jnp.dot(left, right, preferred_element_type=jnp.float32)


def dot_rows(left, right):
    return lax.dot_general(
        left, right, (((0,), (0,)), ((), ())), preferred_element_type=jnp.float32
    )


def dot_back(left, right):
    return lax.dot_general(
        left, right, (((1,), (1,)), ((), ())), preferred_element_type=jnp.float32
    )


def gather_kernel(count, *refs):
    shards, fulls = refs[:count], refs[count : 2 * count]
    own_sem, send_sem, recv_sem = refs[2 * count :]
    me = lax.axis_index("shard")
    core, x, y = me % 2, (me // 2) % 4, me // 8

    def at(dy, dx):
        return (((y + dy) % 2) * 4 + (x + dx) % 4) * 2 + core

    sibling = me + 1 - 2 * core
    right, left, pair = at(0, 1), at(0, 3), at(1, 0)
    barrier = pltpu.get_barrier_semaphore()
    for other in (sibling, right, left, pair):
        pl.semaphore_signal(barrier, inc=1, device_id={"shard": other}, device_id_type=MESH)
    pl.semaphore_wait(barrier, 4)

    began = []

    def send(which, dy, dx, target, half=None):
        rows, width = shards[which].shape
        mine = dy == 0 and dx == 0
        spot = pl.ds(pl.multiple_of(at(dy, dx) * rows, 16), rows)
        cut = pl.ds(0, width) if half is None else pl.ds(half * (width // 2), width // 2)
        source = shards[which].at[:, cut] if mine else fulls[which].at[spot, cut]
        copy = pltpu.make_async_remote_copy(
            src_ref=source,
            dst_ref=fulls[which].at[spot, cut],
            send_sem=send_sem.at[len(began)],
            recv_sem=recv_sem.at[len(began)],
            device_id={"shard": target},
            device_id_type=MESH,
        )
        copy.start()
        began.append(copy)
        return copy

    pair_first = [k for k in range(count) if k not in RING_FIRST]
    ring_first = [k for k in range(count) if k in RING_FIRST]
    kept = []
    for k in range(count):
        rows = shards[k].shape[0]
        spot = pl.ds(pl.multiple_of(me * rows, 16), rows)
        copy = pltpu.make_async_copy(shards[k], fulls[k].at[spot, :], own_sem.at[k])
        copy.start()
        kept.append(copy)
    to_pair, to_right, to_left, shared = {}, {}, {}, []
    for k in pair_first:
        to_pair[k] = send(k, 0, 0, pair)
    for k in ring_first + pair_first:
        to_right[k] = send(k, 0, 0, right)
        to_left[k] = send(k, 0, 0, left)
    for k in ring_first:
        to_pair[k] = send(k, 0, 0, pair)
    for k in range(count):
        shared.append(send(k, 0, 0, sibling))
    pair_right, pair_left = {}, {}
    for k in pair_first:
        to_pair[k].wait_recv()
        pair_right[k] = send(k, 1, 0, right)
        pair_left[k] = send(k, 1, 0, left)
        shared.append(send(k, 1, 0, sibling))
    far, ring_pair = {}, {}
    for k in ring_first + pair_first:
        to_right[k].wait_recv()
        far[k, 0] = send(k, 0, 3, right, 0)
        if k in ring_first:
            ring_pair[k, 3] = send(k, 0, 3, pair)
        shared.append(send(k, 0, 3, sibling))
        to_left[k].wait_recv()
        far[k, 1] = send(k, 0, 1, left, 1)
        if k in ring_first:
            ring_pair[k, 1] = send(k, 0, 1, pair)
        shared.append(send(k, 0, 1, sibling))
    for k in ring_first:
        to_pair[k].wait_recv()
        shared.append(send(k, 1, 0, sibling))
    for k in ring_first:
        far[k, 0].wait_recv()
        far[k, 1].wait_recv()
        ring_pair[k, 2] = send(k, 0, 2, pair)
        shared.append(send(k, 0, 2, sibling))
    far_pair = {}
    for k in pair_first:
        pair_right[k].wait_recv()
        far_pair[k, 0] = send(k, 1, 3, right, 0)
        shared.append(send(k, 1, 3, sibling))
        pair_left[k].wait_recv()
        far_pair[k, 1] = send(k, 1, 1, left, 1)
        shared.append(send(k, 1, 1, sibling))
    for k in pair_first:
        far[k, 0].wait_recv()
        far[k, 1].wait_recv()
        shared.append(send(k, 0, 2, sibling))
    for k in ring_first:
        for dx in (3, 1):
            ring_pair[k, dx].wait_recv()
            shared.append(send(k, 1, dx, sibling))
    for k in pair_first:
        far_pair[k, 0].wait_recv()
        far_pair[k, 1].wait_recv()
        shared.append(send(k, 1, 2, sibling))
    for k in ring_first:
        ring_pair[k, 2].wait_recv()
        shared.append(send(k, 1, 2, sibling))
    for copy in shared:
        copy.wait_recv()
    for copy in began:
        copy.wait_send()
    for copy in kept:
        copy.wait()


def gather_all(arrays):
    count = len(arrays)
    copies = sum(16 if k in RING_FIRST else 17 for k in range(count))
    return pl.pallas_call(
        functools.partial(gather_kernel, count),
        out_shape=[jax.ShapeDtypeStruct((16 * a.shape[0], a.shape[1]), a.dtype) for a in arrays],
        in_specs=[pl.BlockSpec(memory_space=pl.ANY)] * count,
        out_specs=[pl.BlockSpec(memory_space=pl.ANY)] * count,
        scratch_shapes=[
            pltpu.SemaphoreType.DMA((count,)),
            pltpu.SemaphoreType.DMA((copies,)),
            pltpu.SemaphoreType.DMA((copies,)),
        ],
        compiler_params=pltpu.CompilerParams(collective_id=0, has_side_effects=True),
    )(*arrays)


def reduce_kernel(plans, *refs):
    count = len(plans)
    refs = list(refs)

    def take(number):
        taken = refs[:number]
        del refs[:number]
        return taken

    lefts, rights = take(count), take(count)
    outs = take(count)
    sums, from_sibling, to_sibling = take(count), take(count), take(count)
    half_left, half_right, full_left, full_right, from_pair = (take(count) for _ in range(5))
    quarters, merged, spread = take(count), take(count), take(count)
    send_sem, recv_sem = refs

    me, plane = lax.axis_index("shard"), lax.axis_index("dp")
    core, x, y = me % 2, (me // 2) % 4, me // 8

    def chip(dy, dx):
        return ((y + dy) % 2) * 4 + (x + dx) % 4

    sibling = me + 1 - 2 * core
    right, left, pair = (chip(0, 1) * 2 + core, chip(0, 3) * 2 + core, chip(1, 0) * 2 + core)
    barrier = pltpu.get_barrier_semaphore()
    neighbours = [{"shard": d} for d in (sibling, right, left, pair)]
    neighbours += [{"dp": (plane + k) % 4} for k in (1, 2, 3)]
    for other in neighbours:
        pl.semaphore_signal(barrier, inc=1, device_id=other, device_id_type=MESH)
    pl.semaphore_wait(barrier, len(neighbours))

    began = []

    def send(source, target, device):
        copy = pltpu.make_async_remote_copy(
            src_ref=source,
            dst_ref=target,
            send_sem=send_sem.at[len(began)],
            recv_sem=recv_sem.at[len(began)],
            device_id=device,
            device_id_type=MESH,
        )
        copy.start()
        began.append(copy)
        return copy

    def tiles(width, body, tile=512):
        tile = min(tile, width)

        @pl.loop(0, width // tile)
        def _(step):
            body(pl.ds(pl.multiple_of(step * tile, 128), tile))

    def add(where, *others):
        def body(cut):
            total = where[:, cut].astype(jnp.float32)
            for other in others:
                total = total + other[:, cut].astype(jnp.float32)
            where[:, cut] = total.astype(where.dtype)

        tiles(where.shape[1], body)

    width = [p.width for p in plans]
    lower = [pl.ds(0, w // 2) for w in width]
    upper = [pl.ds(w // 2, w // 2) for w in width]
    shared, waiting, slots = {}, [], [[] for _ in range(count)]
    halves, fulls, paired = {}, {}, {}

    def produce(k, dy, dx):
        rows, spot = plans[k].rows, dy * 4 + dx
        place = chip(dy, dx) * 2
        own = pl.ds(pl.multiple_of((place + core) * rows, rows), rows)
        others = pl.ds(pl.multiple_of((place + 1 - core) * rows, rows), rows)
        slot = len(slots[k]) % SLOTS
        if len(slots[k]) >= SLOTS:
            slots[k][-SLOTS].wait_send()
        if plans[k].product:
            both = jnp.concatenate([lefts[k][own, :], lefts[k][others, :]], axis=0)

            def body(cut):
                block = dot(both, rights[k][:, cut])
                sums[k][spot, :, cut] = block[:rows].astype(sums[k].dtype)
                to_sibling[k][slot, :, cut] = block[rows:].astype(sums[k].dtype)

            tiles(width[k], body, 256 if rows > 64 else 512)
        else:
            sums[k][spot] = lefts[k][own, :]
            to_sibling[k][slot] = lefts[k][others, :]
        copy = send(to_sibling[k].at[slot], from_sibling[k].at[spot], {"shard": sibling})
        shared[k, dy, dx] = copy
        slots[k].append(copy)
        waiting.append((k, dy, dx))
        if len(waiting) > 2:
            settle(*waiting[0])

    def send_halves(k, dy):
        part = dy if plans[k].ring_first else 0
        halves[k, dy, 0] = send(
            sums[k].at[dy * 4 + 2, :, lower[k]], half_left[k].at[part], {"shard": right}
        )
        halves[k, dy, 1] = send(
            sums[k].at[dy * 4 + 2, :, upper[k]], half_right[k].at[part], {"shard": left}
        )

    def settle(k, dy, dx):
        if (k, dy, dx) not in waiting:
            return
        waiting.remove((k, dy, dx))
        spot = dy * 4 + dx
        shared[k, dy, dx].wait_recv()
        add(sums[k].at[spot], from_sibling[k].at[spot])
        if plans[k].ring_first:
            if dx == 2:
                send_halves(k, dy)
        elif dy == 1:
            paired[k, dx] = send(sums[k].at[spot], from_pair[k].at[dx], {"shard": pair})

    def forward(k, dy):
        part = dy if plans[k].ring_first else 0
        settle(k, dy, 1)
        halves[k, dy, 0].wait_recv()
        add(sums[k].at[dy * 4 + 1, :, lower[k]], half_left[k].at[part])
        fulls[k, dy, 0] = send(sums[k].at[dy * 4 + 1], full_left[k].at[part], {"shard": right})
        settle(k, dy, 3)
        halves[k, dy, 1].wait_recv()
        add(sums[k].at[dy * 4 + 3, :, upper[k]], half_right[k].at[part])
        fulls[k, dy, 1] = send(sums[k].at[dy * 4 + 3], full_right[k].at[part], {"shard": left})

    def meet(k, dx):
        settle(k, 0, dx)
        paired[k, dx].wait_recv()
        add(sums[k].at[dx], from_pair[k].at[dx])

    def ring_end(k, dy):
        part = dy if plans[k].ring_first else 0
        settle(k, dy, 0)
        fulls[k, dy, 0].wait_recv()
        fulls[k, dy, 1].wait_recv()
        add(sums[k].at[dy * 4], full_left[k].at[part], full_right[k].at[part])

    def cut_of(k, which):
        quarter = width[k] // 4
        return pl.ds(pl.multiple_of(which * quarter, 128), quarter)

    scattered, returned = {}, {}

    def scatter_planes(k):
        for hop in (2, 1, 3):
            there = (plane + hop) % 4
            scattered[k, hop] = send(sums[k].at[0, :, cut_of(k, there)], quarters[k].at[hop - 1], {"dp": there})

    def return_planes(k):
        for hop in (1, 2, 3):
            scattered[k, hop].wait_recv()
        total = sums[k][0, :, cut_of(k, plane)].astype(jnp.float32)
        for hop in range(3):
            total = total + quarters[k][hop].astype(jnp.float32)
        merged[k][...] = total.astype(merged[k].dtype)
        spread[k][:, cut_of(k, plane)] = merged[k][...]
        for hop in (2, 1, 3):
            there = (plane + hop) % 4
            returned[k, hop] = send(merged[k], spread[k].at[:, cut_of(k, plane)], {"dp": there})

    def finish(k):
        for hop in (1, 2, 3):
            returned[k, hop].wait_recv()

        def body(cut):
            outs[k][:, cut] = spread[k][:, cut].astype(jnp.float32)

        tiles(width[k], body)

    down, up, out, joint, vectors = range(5)
    for k, dy, dx in (
        (up, 1, 2), (up, 0, 2), (down, 1, 2), (joint, 1, 2), (joint, 0, 2), (down, 1, 1), (down, 1, 3),
        (down, 1, 0), (vectors, 1, 2), (vectors, 0, 2),
    ):
        produce(k, dy, dx)
    for dy in (1, 0):
        produce(up, dy, 1)
        produce(up, dy, 3)
        forward(up, dy)
    for dx in (2, 1, 3, 0):
        produce(out, 1, dx)
    for dy in (1, 0):
        produce(joint, dy, 1)
        produce(joint, dy, 3)
        forward(joint, dy)
    produce(down, 0, 2)
    meet(down, 2)
    send_halves(down, 0)
    for dy in (1, 0):
        produce(vectors, dy, 1)
        produce(vectors, dy, 3)
        forward(vectors, dy)
    produce(out, 0, 2)
    meet(out, 2)
    send_halves(out, 0)
    produce(up, 1, 0)
    ring_end(up, 1)
    paired[up, 0] = send(sums[up].at[4], from_pair[up].at[0], {"shard": pair})
    for k in (down, out):
        produce(k, 0, 1)
        produce(k, 0, 3)
        meet(k, 1)
        meet(k, 3)
        forward(k, 0)
    for k in (joint, vectors):
        produce(k, 1, 0)
        ring_end(k, 1)
        paired[k, 0] = send(sums[k].at[4], from_pair[k].at[0], {"shard": pair})
    for k in (up, joint, vectors):
        produce(k, 0, 0)
        ring_end(k, 0)
        paired[k, 0].wait_recv()
        add(sums[k].at[0], from_pair[k].at[0])
        scatter_planes(k)
    return_planes(up)
    for k in (down, out):
        produce(k, 0, 0)
        meet(k, 0)
        ring_end(k, 0)
        scatter_planes(k)
    for k in (joint, vectors, down, out):
        return_planes(k)
    for k in (up, joint, vectors, down, out):
        finish(k)
    kept_back = {id(c) for per in slots for c in per[:-SLOTS]}
    for copy in began:
        if id(copy) not in kept_back:
            copy.wait_send()


Plan = collections.namedtuple("Plan", ("rows", "width", "product", "ring_first", "dtype"))
SLOTS = 3


def reduce_all(pairs, vectors):
    plans = [
        Plan(left.shape[0] // 16, right.shape[1], True, k in (1, 3), jnp.bfloat16)
        for k, (left, right) in enumerate(pairs)
    ]
    plans.append(Plan(vectors.shape[0] // 16, vectors.shape[1], False, True, jnp.float32))
    lefts = [left for left, _ in pairs] + [vectors]
    rights = [right for _, right in pairs] + [jnp.zeros((8, 128), jnp.float32)]

    def room(depth, part=1):
        return [
            pltpu.VMEM((depth(p) if callable(depth) else depth, p.rows, p.width // part), p.dtype) for p in plans
        ]

    ring_parts = lambda p: 2 if p.ring_first else 1
    scratch = room(8) + room(8) + room(SLOTS)
    scratch += room(ring_parts, 2) + room(ring_parts, 2) + room(ring_parts) + room(ring_parts)
    scratch += room(lambda p: 1 if p.ring_first else 4)
    scratch += room(3, 4)
    scratch += [pltpu.VMEM((p.rows, p.width // 4), p.dtype) for p in plans]
    scratch += [pltpu.VMEM((p.rows, p.width), p.dtype) for p in plans]
    copies = sum(8 + (9 if p.ring_first else 8) + 6 for p in plans)
    return pl.pallas_call(
        functools.partial(reduce_kernel, plans),
        out_shape=[jax.ShapeDtypeStruct((p.rows, p.width), jnp.float32) for p in plans],
        in_specs=[pl.BlockSpec(memory_space=pltpu.VMEM)] * (2 * len(plans)),
        out_specs=[pl.BlockSpec(memory_space=pltpu.VMEM)] * len(plans),
        scratch_shapes=scratch
        + [pltpu.SemaphoreType.DMA((copies,)), pltpu.SemaphoreType.DMA((copies,))],
        compiler_params=pltpu.CompilerParams(
            collective_id=1, has_side_effects=True, vmem_limit_bytes=62 * 1024 * 1024
        ),
    )(*lefts, *rights)


def relay_kernel(
    rows, cotangent, allowed, vec, bias_qkv, bias_up, hbm_qkv, hbm_out, hbm_up, hbm_down,
    section_out, section_grad, hidden_t, second_t, attended_t, normed_t, du, dbefore, db, dprojected, sums, sum_up,
    w_qkv, w_out, w_up, w_down, x, hat_one, scale_one, normed, qkv, probs, attended, middle, hat_two, scale_two,
    second, slope, hidden, wide, dmiddle, dattended, ship_out, ship_grad, land_out, land_grad,
    load_sem, send_sem, recv_sem,
):
    section = lax.axis_index("section")
    first = section == 0
    loads = [
        pltpu.make_async_copy(source, target, load_sem.at[k])
        for k, (source, target) in enumerate(
            ((hbm_qkv, w_qkv), (hbm_out, w_out), (hbm_up, w_up), (hbm_down, w_down))
        )
    ]
    for load in loads:
        load.start()
    barrier = pltpu.get_barrier_semaphore()
    pl.semaphore_signal(barrier, inc=1, device_id={"section": 1 - section}, device_id_type=MESH)
    pl.semaphore_wait(barrier, 1)

    def hop(source, target, k):
        return pltpu.make_async_remote_copy(
            src_ref=source, dst_ref=target, send_sem=send_sem.at[k], recv_sem=recv_sem.at[k],
            device_id={"section": 1 - section}, device_id_type=MESH,
        )

    def tiles(width, body, tile=512):
        @pl.loop(0, width // tile)
        def _(step):
            body(pl.ds(pl.multiple_of(step * tile, 128), tile))

    ln1_gain, ln1_bias, _, _, b_out, ln2_gain, ln2_bias, b_down = (vec[k : k + 1, :] for k in range(8))
    lane = lax.broadcasted_iota(jnp.int32, (SLOT, 128), 1)
    low_half = lane < 64
    halves = (low_half, jnp.logical_not(low_half))

    def standard(values):
        centered = values - jnp.mean(values, axis=-1, keepdims=True)
        scale = lax.rsqrt(jnp.mean(centered * centered, axis=-1, keepdims=True) + norm_eps)
        return centered * scale, scale

    def only(which, values):
        return jnp.where(halves[which], values, jnp.zeros_like(values))

    def forward(result, before_use):
        hat, scale = standard(x[...].astype(jnp.float32))
        hat_one[...] = hat
        scale_one[...] = scale
        normed[...] = (hat * ln1_gain + ln1_bias).astype(jnp.bfloat16)
        before_use(0)

        def project(cut):
            qkv[:, cut] = (dot(normed[...], w_qkv[:, cut]) + bias_qkv[:, cut]).astype(jnp.bfloat16)

        tiles(3072, project)

        @pl.loop(0, HEADS // 2)
        def _(couple):
            cuts = [pl.ds(pl.multiple_of(couple * 128 + 1024 * k, 128), 128) for k in range(3)]
            for slot in range(2):
                spot = pl.ds(slot * SLOT, SLOT)
                query, key, value = (qkv[spot, cut] for cut in cuts)
                mixed = []
                for which in range(2):
                    scores = dot_back(query, only(which, key)) * 0.125
                    scores = jnp.where(allowed[slot] > 0, scores, masked_score)
                    exponent = jnp.exp(scores - jnp.max(scores, axis=-1, keepdims=True))
                    prob = exponent / jnp.sum(exponent, axis=-1, keepdims=True)
                    probs[couple * 4 + slot * 2 + which] = prob
                    mixed.append(dot(prob.astype(jnp.bfloat16), value))
                attended[spot, cuts[0]] = jnp.where(low_half, *mixed).astype(jnp.bfloat16)

        before_use(1)

        def mix(cut):
            branch = dot(attended[...], w_out[:, cut]) + vec[4:5, cut]
            middle[:, cut] = x[:, cut].astype(jnp.float32) + branch

        tiles(1024, mix)
        hat, scale = standard(middle[...])
        hat_two[...] = hat
        scale_two[...] = scale
        second[...] = (hat * ln2_gain + ln2_bias).astype(jnp.bfloat16)
        before_use(2)

        def grow(cut):
            before = dot(second[...], w_up[:, cut]) + bias_up[:, cut]
            square = before * before
            bend = jnp.tanh(GELU_A * (before + GELU_B * before * square))
            half = 0.5 * (1.0 + bend)
            hidden[:, cut] = (before * half).astype(jnp.bfloat16)
            slope[:, cut] = half + (0.5 * GELU_A) * before * (1.0 - bend * bend) * (1.0 + (3.0 * GELU_B) * square)

        tiles(4096, grow, 256)
        before_use(3)

        def shrink(cut):
            result[:, cut] = (middle[:, cut] + dot(hidden[...], w_down[:, cut]) + vec[7:8, cut]).astype(jnp.bfloat16)

        tiles(1024, shrink)

    def norm_back(hat, scale, grad, gain):
        inner = grad * gain
        return scale * (
            inner
            - jnp.mean(inner, axis=-1, keepdims=True)
            - hat * jnp.mean(inner * hat, axis=-1, keepdims=True)
        )

    def total(values):
        return jnp.sum(values.astype(jnp.float32), axis=0, keepdims=True)

    def backward(result, last):
        def grow_back(cut):
            grad = dot_back(du[...], w_down[cut, :]) * slope[:, cut]
            dbefore[:, cut] = grad.astype(jnp.bfloat16)
            if last:
                sum_up[:, cut] = total(dbefore[:, cut])

        tiles(4096, grow_back)

        def second_back(cut):
            wide[:, cut] = dot_back(dbefore[...], w_up[cut, :])

        tiles(1024, second_back)
        grad = wide[...]
        if last:
            sums[5:6, :] = jnp.sum(grad * hat_two[...], axis=0, keepdims=True)
            sums[6:7, :] = total(grad)
            sums[7:8, :] = total(du[...])
        dmiddle[...] = du[...].astype(jnp.float32) + norm_back(hat_two[...], scale_two[...], grad, ln2_gain)
        db[...] = dmiddle[...].astype(jnp.bfloat16)

        def mix_back(cut):
            dattended[:, cut] = dot_back(db[...], w_out[cut, :]).astype(jnp.bfloat16)

        tiles(1024, mix_back)

        @pl.loop(0, HEADS // 2)
        def _(couple):
            cuts = [pl.ds(pl.multiple_of(couple * 128 + 1024 * k, 128), 128) for k in range(3)]
            for slot in range(2):
                spot = pl.ds(slot * SLOT, SLOT)
                query, key, value = (qkv[spot, cut] for cut in cuts)
                grad = dattended[spot, cuts[0]]
                parts = ([], [], [])
                for which in range(2):
                    prob = probs[couple * 4 + slot * 2 + which]
                    dprob = dot_back(only(which, grad), value)
                    delta = jnp.sum(prob * dprob, axis=-1, keepdims=True)
                    dscore = (prob * (dprob - delta)).astype(jnp.bfloat16)
                    parts[0].append(dot(dscore, key) * 0.125)
                    parts[1].append(dot_rows(dscore, query) * 0.125)
                    parts[2].append(dot_rows(prob.astype(jnp.bfloat16), grad))
                for cut, part in zip(cuts, parts):
                    dprojected[spot, cut] = jnp.where(low_half, *part).astype(jnp.bfloat16)

        def normed_back(cut):
            wide[:, cut] = dot_back(dprojected[...], w_qkv[cut, :])

        tiles(1024, normed_back)
        grad = wide[...]
        result[...] = (dmiddle[...] + norm_back(hat_one[...], scale_one[...], grad, ln1_gain)).astype(jnp.bfloat16)
        if last:
            sums[0:1, :] = jnp.sum(grad * hat_one[...], axis=0, keepdims=True)
            sums[1:2, :] = total(grad)
            sums[2:3, :] = total(dprojected[:, :1024])
            sums[3:4, :] = total(dprojected[:, 2048:])
            sums[4:5, :] = total(db[...])

    x[...] = rows[...]
    forward(ship_out, lambda k: loads[k].wait())
    there = hop(ship_out, land_out, 0)
    there.start()
    there.wait()
    x[...] = jnp.where(first, rows[...], land_out[...])
    forward(section_out, lambda k: None)
    du[...] = cotangent[...]
    backward(ship_grad, False)
    back = hop(ship_grad, land_grad, 1)
    back.start()

    def flip(source, target):
        def body(cut):
            target[cut, :] = source[:, cut].T

        tiles(source.shape[1], body, 256)

    for source, target in ((hidden, hidden_t), (second, second_t), (attended, attended_t), (normed, normed_t)):
        flip(source, target)
    back.wait()
    du[...] = jnp.where(first, land_grad[...], cotangent[...])
    backward(section_grad, True)


def relay(rows, cotangent, allowed, vec, bias_qkv, bias_up, mats):
    tall, width, wide = rows.shape[0], rows.shape[1], mats[2].shape[1]
    low, full = jnp.bfloat16, jnp.float32
    outs = [
        ((tall, width), low), ((tall, width), low), ((wide, tall), low), ((width, tall), low), ((width, tall), low),
        ((width, tall), low), ((tall, width), low), ((tall, wide), low), ((tall, width), low),
        ((tall, 3 * width), low), ((8, width), full), ((1, wide), full),
    ]
    scratch = [(m.shape, low) for m in mats] + [
        ((tall, width), low), ((tall, width), full), ((tall, 1), full), ((tall, width), low),
        ((tall, 3 * width), low), ((2 * HEADS, SLOT, SLOT), full), ((tall, width), low), ((tall, width), full),
        ((tall, width), full), ((tall, 1), full), ((tall, width), low), ((tall, wide), full), ((tall, wide), low),
        ((tall, width), full), ((tall, width), full), ((tall, width), low),
    ] + [((tall, width), low)] * 4
    in_vmem, anywhere = pl.BlockSpec(memory_space=pltpu.VMEM), pl.BlockSpec(memory_space=pl.ANY)
    return pl.pallas_call(
        relay_kernel,
        out_shape=[jax.ShapeDtypeStruct(*o) for o in outs],
        in_specs=[in_vmem] * 6 + [anywhere] * 4,
        out_specs=[in_vmem] * len(outs),
        scratch_shapes=[pltpu.VMEM(*s) for s in scratch]
        + [pltpu.SemaphoreType.DMA((n,)) for n in (4, 2, 2)],
        compiler_params=pltpu.CompilerParams(
            collective_id=2, has_side_effects=True, vmem_limit_bytes=62 * 1024 * 1024
        ),
    )(rows, cotangent, allowed, vec, bias_qkv, bias_up, *mats)


def allowed_pairs(segment):
    by_slot = segment.reshape(-1, SLOT)
    positions = jnp.arange(SLOT)
    allowed = (by_slot[:, :, None] == by_slot[:, None, :]) & (positions[None, :] <= positions[:, None])
    return allowed.astype(jnp.float32)


def on_device(
    ends, segment_ids, token_mask,
    ln1_gain, ln1_bias, w_qkv, b_query, b_value, w_out, b_out,
    ln2_gain, ln2_bias, w_up, b_up, w_down, b_down,
):
    width = ends.shape[2]
    shard_count = lax.axis_size("shard")
    packed = jnp.concatenate([ln1_gain, ln1_bias, b_query, b_value, b_out, ln2_gain, ln2_bias, b_down, b_up], axis=1)
    tall = jnp.broadcast_to(packed, (16, packed.shape[1]))
    *mats, everyone = gather_all((w_qkv[0], w_out[0], w_up[0], w_down[0], tall))
    everyone = everyone.reshape(shard_count, *tall.shape)[:, 0].astype(jnp.float32)
    piece = width // shard_count
    vec = everyone[:, : 8 * piece].reshape(shard_count, 8, piece).transpose(1, 0, 2).reshape(8, width)
    bias_up = everyone[:, 8 * piece :].reshape(1, -1)
    bias_qkv = jnp.concatenate([vec[2:3], jnp.zeros((1, width), jnp.float32), vec[3:4]], axis=1)

    local_rows = ends[0]
    cotangent = local_rows * token_mask[:, None].astype(jnp.bfloat16)
    (
        section_out, section_grad, hidden_t, second_t, attended_t, normed_t, du, dbefore, db, dprojected, sums, sum_up,
    ) = relay(local_rows, cotangent, allowed_pairs(segment_ids), vec, bias_qkv, bias_up, mats)

    rows = jnp.concatenate(
        [
            sums.reshape(8, shard_count, piece).transpose(1, 0, 2).reshape(shard_count, 8 * piece),
            sum_up.reshape(shard_count, -1),
        ],
        axis=1,
    )
    spread = jnp.pad(rows[:, None], ((0, 0), (0, 7), (0, 1024 - rows.shape[1])))
    g_down, g_up, g_out, g_qkv, mine = reduce_all(
        ((hidden_t, du), (second_t, dbefore), (attended_t, db), (normed_t, dprojected)), spread.reshape(-1, 1024)
    )
    out = [mine[:1, k * piece : (k + 1) * piece] for k in range(8)]
    g_ln1_gain, g_ln1_bias, g_query, g_value, g_b_out, g_ln2_gain, g_ln2_bias, g_b_down = out
    g_b_up = mine[:1, 8 * piece : 8 * piece + b_up.shape[1]]
    return (
        section_out[None], section_grad[None], g_ln1_gain, g_ln1_bias, g_qkv[None], g_query, g_value, g_out[None],
        g_b_out, g_ln2_gain, g_ln2_bias, g_up[None], g_b_up, g_down[None], g_b_down,
    )


def solution(mesh):
    vector, matrix = P("section", "shard"), P("section", "shard", None)
    rows, ids = P("section", ("dp", "shard"), None), P(("dp", "shard"))
    in_specs = (
        rows, ids, ids, vector, vector, matrix, vector, vector, matrix, vector, vector, vector, matrix,
        vector, matrix, vector,
    )
    out_specs = (
        rows, rows, vector, vector, matrix, vector, vector, matrix, vector, vector, vector, matrix, vector,
        matrix, vector,
    )
    return jax.shard_map(on_device, mesh=mesh, in_specs=in_specs, out_specs=out_specs, check_vma=False)
```

```python
import collections
import functools
import math

import jax
import jax.numpy as jnp
import numpy as np
from jax import lax
from jax.experimental import pallas as pl
from jax.experimental.pallas import tpu as pltpu
from jax.sharding import PartitionSpec as P

HEADS = 16
SLOT = 96
GELU_A = math.sqrt(2.0 / math.pi)
GELU_B = 0.044715

norm_eps = 1e-05
masked_score = -1e30
MESH = pl.DeviceIdType.MESH
SCALE = np.array(0.125, jnp.bfloat16)
RING_FIRST = (3,)
SPREAD = 2
FIRST_USED = (2, 4, 0, 1, 3)


def dot(left, right):
    return jnp.dot(left, right, preferred_element_type=jnp.float32)


def dot_rows(left, right):
    return lax.dot_general(
        left, right, (((0,), (0,)), ((), ())), preferred_element_type=jnp.float32
    )


def dot_back(left, right):
    return lax.dot_general(
        left, right, (((1,), (1,)), ((), ())), preferred_element_type=jnp.float32
    )


def gather_kernel(count, *refs):
    shards, fulls = refs[:count], refs[count : 2 * count]
    own_sem, send_sem, recv_sem = refs[2 * count :]
    me, plane = lax.axis_index("shard"), lax.axis_index("dp")
    core, x, y = me % 2, (me // 2) % 4, me // 8

    def at(dy, dx):
        return (((y + dy) % 2) * 4 + (x + dx) % 4) * 2 + core

    sibling = me + 1 - 2 * core
    right, left, pair = at(0, 1), at(0, 3), at(1, 0)
    barrier = pltpu.get_barrier_semaphore()
    neighbours = [{"shard": d} for d in (sibling, right, left, pair)]
    neighbours += [{"dp": (plane + k) % 4} for k in (1, 2, 3)]
    for other in neighbours:
        pl.semaphore_signal(barrier, inc=1, device_id=other, device_id_type=MESH)
    pl.semaphore_wait(barrier, len(neighbours))

    began = []

    def send(which, dy, dx, target, half=None, whole=False):
        rows, width = shards[which].shape
        mine = dy == 0 and dx == 0
        spot = pl.ds(pl.multiple_of(at(dy, dx) * rows, 16), rows)
        start = 0
        if which == SPREAD and not whole:
            width = width // 4
            start = pl.multiple_of(plane * width, 128)
        cut = pl.ds(start, width)
        if half is not None:
            cut = pl.ds(start + half * (width // 2), width // 2)
        source = shards[which].at[:, cut] if mine else fulls[which].at[spot, cut]
        copy = pltpu.make_async_remote_copy(
            src_ref=source,
            dst_ref=fulls[which].at[spot, cut],
            send_sem=send_sem.at[len(began)],
            recv_sem=recv_sem.at[len(began)],
            device_id=target if isinstance(target, dict) else {"shard": target},
            device_id_type=MESH,
        )
        copy.start()
        began.append(copy)
        return copy

    spreads = []

    def share(which, dy, dx):
        if which == SPREAD and (dy, dx) != (0, 0):
            copies = [send(which, dy, dx, {"dp": (plane + k) % 4}) for k in (2, 1, 3)]
            spreads.append((dy, dx, copies))
        else:
            shared.append(send(which, dy, dx, sibling, whole=True))

    pair_first = [k for k in FIRST_USED if k not in RING_FIRST]
    ring_first = [k for k in FIRST_USED if k in RING_FIRST]
    kept = []
    for k in range(count):
        rows = shards[k].shape[0]
        spot = pl.ds(pl.multiple_of(me * rows, 16), rows)
        copy = pltpu.make_async_copy(shards[k], fulls[k].at[spot, :], own_sem.at[k])
        copy.start()
        kept.append(copy)
    to_pair, to_right, to_left, shared = {}, {}, {}, []
    for k in pair_first:
        to_pair[k] = send(k, 0, 0, pair)
    for k in ring_first + pair_first:
        to_right[k] = send(k, 0, 0, right)
        to_left[k] = send(k, 0, 0, left)
    for k in ring_first:
        to_pair[k] = send(k, 0, 0, pair)
    for k in range(count):
        share(k, 0, 0)
    pair_right, pair_left = {}, {}
    for k in pair_first:
        to_pair[k].wait_recv()
        pair_right[k] = send(k, 1, 0, right)
        pair_left[k] = send(k, 1, 0, left)
        share(k, 1, 0)
    far, ring_pair = {}, {}
    for k in ring_first + pair_first:
        to_right[k].wait_recv()
        far[k, 0] = send(k, 0, 3, right, 0)
        if k in ring_first:
            ring_pair[k, 3] = send(k, 0, 3, pair)
        share(k, 0, 3)
        to_left[k].wait_recv()
        far[k, 1] = send(k, 0, 1, left, 1)
        if k in ring_first:
            ring_pair[k, 1] = send(k, 0, 1, pair)
        share(k, 0, 1)
    for k in ring_first:
        to_pair[k].wait_recv()
        share(k, 1, 0)
    for k in ring_first:
        far[k, 0].wait_recv()
        far[k, 1].wait_recv()
        ring_pair[k, 2] = send(k, 0, 2, pair)
        share(k, 0, 2)
    far_pair = {}
    for k in pair_first:
        pair_right[k].wait_recv()
        far_pair[k, 0] = send(k, 1, 3, right, 0)
        share(k, 1, 3)
        pair_left[k].wait_recv()
        far_pair[k, 1] = send(k, 1, 1, left, 1)
        share(k, 1, 1)
    for k in pair_first:
        far[k, 0].wait_recv()
        far[k, 1].wait_recv()
        share(k, 0, 2)
    for k in ring_first:
        for dx in (3, 1):
            ring_pair[k, dx].wait_recv()
            share(k, 1, dx)
    for k in pair_first:
        far_pair[k, 0].wait_recv()
        far_pair[k, 1].wait_recv()
        share(k, 1, 2)
    for k in ring_first:
        ring_pair[k, 2].wait_recv()
        share(k, 1, 2)
    for dy, dx, copies in spreads:
        for copy in copies:
            copy.wait_recv()
        shared.append(send(SPREAD, dy, dx, sibling, whole=True))
    for copy in shared:
        copy.wait_recv()
    for copy in began:
        copy.wait_send()
    for copy in kept:
        copy.wait()


def gather_all(arrays):
    count = len(arrays)
    copies = sum(16 if k in RING_FIRST else 17 for k in range(count)) + 21
    return pl.pallas_call(
        functools.partial(gather_kernel, count),
        out_shape=[jax.ShapeDtypeStruct((16 * a.shape[0], a.shape[1]), a.dtype) for a in arrays],
        in_specs=[pl.BlockSpec(memory_space=pl.ANY)] * count,
        out_specs=[pl.BlockSpec(memory_space=pl.ANY)] * count,
        scratch_shapes=[
            pltpu.SemaphoreType.DMA((count,)),
            pltpu.SemaphoreType.DMA((copies,)),
            pltpu.SemaphoreType.DMA((copies,)),
        ],
        compiler_params=pltpu.CompilerParams(collective_id=0, has_side_effects=True),
    )(*arrays)


def reduce_kernel(plans, *refs):
    count = len(plans)
    refs = list(refs)

    def take(number):
        taken = refs[:number]
        del refs[:number]
        return taken

    lefts, rights = take(count), take(count)
    outs = take(count)
    sums, from_sibling, to_sibling = take(count), take(count), take(count)
    half_left, half_right, full_left, full_right, from_pair = (take(count) for _ in range(5))
    quarters, merged, spread = take(count), take(count), take(count)
    send_sem, recv_sem = refs

    me, plane = lax.axis_index("shard"), lax.axis_index("dp")
    core, x, y = me % 2, (me // 2) % 4, me // 8

    def chip(dy, dx):
        return ((y + dy) % 2) * 4 + (x + dx) % 4

    sibling = me + 1 - 2 * core
    right, left, pair = (chip(0, 1) * 2 + core, chip(0, 3) * 2 + core, chip(1, 0) * 2 + core)
    barrier = pltpu.get_barrier_semaphore()
    neighbours = [{"shard": d} for d in (sibling, right, left, pair)]
    neighbours += [{"dp": (plane + k) % 4} for k in (1, 2, 3)]
    for other in neighbours:
        pl.semaphore_signal(barrier, inc=1, device_id=other, device_id_type=MESH)
    pl.semaphore_wait(barrier, len(neighbours))

    began = []

    def send(source, target, device):
        copy = pltpu.make_async_remote_copy(
            src_ref=source,
            dst_ref=target,
            send_sem=send_sem.at[len(began)],
            recv_sem=recv_sem.at[len(began)],
            device_id=device,
            device_id_type=MESH,
        )
        copy.start()
        began.append(copy)
        return copy

    def tiles(width, body, tile=512):
        tile = min(tile, width)

        @pl.loop(0, width // tile)
        def _(step):
            body(pl.ds(pl.multiple_of(step * tile, 128), tile))

    def add(where, *others):
        def body(cut):
            total = where[:, cut].astype(jnp.float32)
            for other in others:
                total = total + other[:, cut].astype(jnp.float32)
            where[:, cut] = total.astype(where.dtype)

        tiles(where.shape[1], body)

    width = [p.width for p in plans]
    lower = [pl.ds(0, w // 2) for w in width]
    upper = [pl.ds(w // 2, w // 2) for w in width]
    shared, waiting, slots = {}, [], [[] for _ in range(count)]
    halves, fulls, paired = {}, {}, {}

    def produce(k, dy, dx):
        rows, spot = plans[k].rows, dy * 4 + dx
        place = chip(dy, dx) * 2
        own = pl.ds(pl.multiple_of((place + core) * rows, rows), rows)
        others = pl.ds(pl.multiple_of((place + 1 - core) * rows, rows), rows)
        slot = len(slots[k]) % SLOTS
        if len(slots[k]) >= SLOTS:
            slots[k][-SLOTS].wait_send()
        if plans[k].product:
            both = jnp.concatenate([lefts[k][own, :], lefts[k][others, :]], axis=0)

            def body(cut):
                block = dot(both, rights[k][:, cut])
                sums[k][spot, :, cut] = block[:rows].astype(sums[k].dtype)
                to_sibling[k][slot, :, cut] = block[rows:].astype(sums[k].dtype)

            tiles(width[k], body, 256 if rows > 64 else 512)
        else:
            sums[k][spot] = lefts[k][own, :]
            to_sibling[k][slot] = lefts[k][others, :]
        copy = send(to_sibling[k].at[slot], from_sibling[k].at[spot], {"shard": sibling})
        shared[k, dy, dx] = copy
        slots[k].append(copy)
        waiting.append((k, dy, dx))
        if len(waiting) > 2:
            settle(*waiting[0])

    def send_halves(k, dy):
        part = dy if plans[k].ring_first else 0
        halves[k, dy, 0] = send(
            sums[k].at[dy * 4 + 2, :, lower[k]], half_left[k].at[part], {"shard": right}
        )
        halves[k, dy, 1] = send(
            sums[k].at[dy * 4 + 2, :, upper[k]], half_right[k].at[part], {"shard": left}
        )

    def settle(k, dy, dx):
        if (k, dy, dx) not in waiting:
            return
        waiting.remove((k, dy, dx))
        spot = dy * 4 + dx
        shared[k, dy, dx].wait_recv()
        add(sums[k].at[spot], from_sibling[k].at[spot])
        if plans[k].ring_first:
            if dx == 2:
                send_halves(k, dy)
        elif dy == 1:
            paired[k, dx] = send(sums[k].at[spot], from_pair[k].at[dx], {"shard": pair})

    def forward(k, dy):
        part = dy if plans[k].ring_first else 0
        settle(k, dy, 1)
        halves[k, dy, 0].wait_recv()
        add(sums[k].at[dy * 4 + 1, :, lower[k]], half_left[k].at[part])
        fulls[k, dy, 0] = send(sums[k].at[dy * 4 + 1], full_left[k].at[part], {"shard": right})
        settle(k, dy, 3)
        halves[k, dy, 1].wait_recv()
        add(sums[k].at[dy * 4 + 3, :, upper[k]], half_right[k].at[part])
        fulls[k, dy, 1] = send(sums[k].at[dy * 4 + 3], full_right[k].at[part], {"shard": left})

    def meet(k, dx):
        settle(k, 0, dx)
        paired[k, dx].wait_recv()
        add(sums[k].at[dx], from_pair[k].at[dx])

    def ring_end(k, dy):
        part = dy if plans[k].ring_first else 0
        settle(k, dy, 0)
        fulls[k, dy, 0].wait_recv()
        fulls[k, dy, 1].wait_recv()
        add(sums[k].at[dy * 4], full_left[k].at[part], full_right[k].at[part])

    def cut_of(k, which):
        quarter = width[k] // 4
        return pl.ds(pl.multiple_of(which * quarter, 128), quarter)

    scattered, returned = {}, {}

    def scatter_planes(k):
        for hop in (2, 1, 3):
            there = (plane + hop) % 4
            scattered[k, hop] = send(sums[k].at[0, :, cut_of(k, there)], quarters[k].at[hop - 1], {"dp": there})

    def return_planes(k):
        for hop in (1, 2, 3):
            scattered[k, hop].wait_recv()
        total = sums[k][0, :, cut_of(k, plane)].astype(jnp.float32)
        for hop in range(3):
            total = total + quarters[k][hop].astype(jnp.float32)
        merged[k][...] = total.astype(merged[k].dtype)
        spread[k][:, cut_of(k, plane)] = merged[k][...]
        for hop in (2, 1, 3):
            there = (plane + hop) % 4
            returned[k, hop] = send(merged[k], spread[k].at[:, cut_of(k, plane)], {"dp": there})

    def finish(k):
        for hop in (1, 2, 3):
            returned[k, hop].wait_recv()

        def body(cut):
            outs[k][:, cut] = spread[k][:, cut].astype(jnp.float32)

        tiles(width[k], body)

    down, up, out, joint, vectors = range(5)
    for k, dy, dx in (
        (up, 1, 2), (up, 0, 2), (down, 1, 2), (joint, 1, 2), (joint, 0, 2), (down, 1, 1), (down, 1, 3),
        (down, 1, 0), (vectors, 1, 2), (vectors, 0, 2),
    ):
        produce(k, dy, dx)
    for dy in (1, 0):
        produce(up, dy, 1)
        produce(up, dy, 3)
        forward(up, dy)
    for dx in (2, 1, 3, 0):
        produce(out, 1, dx)
    for dy in (1, 0):
        produce(joint, dy, 1)
        produce(joint, dy, 3)
        forward(joint, dy)
    produce(down, 0, 2)
    meet(down, 2)
    send_halves(down, 0)
    for dy in (1, 0):
        produce(vectors, dy, 1)
        produce(vectors, dy, 3)
        forward(vectors, dy)
    produce(out, 0, 2)
    meet(out, 2)
    send_halves(out, 0)
    produce(up, 1, 0)
    ring_end(up, 1)
    paired[up, 0] = send(sums[up].at[4], from_pair[up].at[0], {"shard": pair})
    for k in (down, out):
        produce(k, 0, 1)
        produce(k, 0, 3)
        meet(k, 1)
        meet(k, 3)
        forward(k, 0)
    for k in (joint, vectors):
        produce(k, 1, 0)
        ring_end(k, 1)
        paired[k, 0] = send(sums[k].at[4], from_pair[k].at[0], {"shard": pair})
    for k in (up, joint, vectors):
        produce(k, 0, 0)
        ring_end(k, 0)
        paired[k, 0].wait_recv()
        add(sums[k].at[0], from_pair[k].at[0])
        scatter_planes(k)
    return_planes(up)
    for k in (down, out):
        produce(k, 0, 0)
        meet(k, 0)
        ring_end(k, 0)
        scatter_planes(k)
    for k in (joint, vectors, down, out):
        return_planes(k)
    for k in (up, joint, vectors, down, out):
        finish(k)
    kept_back = {id(c) for per in slots for c in per[:-SLOTS]}
    for copy in began:
        if id(copy) not in kept_back:
            copy.wait_send()


Plan = collections.namedtuple("Plan", ("rows", "width", "product", "ring_first", "dtype"))
SLOTS = 3


def reduce_all(pairs, vectors):
    plans = [
        Plan(left.shape[0] // 16, right.shape[1], True, k in (1, 3), jnp.bfloat16)
        for k, (left, right) in enumerate(pairs)
    ]
    plans.append(Plan(vectors.shape[0] // 16, vectors.shape[1], False, True, jnp.float32))
    lefts = [left for left, _ in pairs] + [vectors]
    rights = [right for _, right in pairs] + [jnp.zeros((8, 128), jnp.float32)]

    def room(depth, part=1):
        return [
            pltpu.VMEM((depth(p) if callable(depth) else depth, p.rows, p.width // part), p.dtype) for p in plans
        ]

    ring_parts = lambda p: 2 if p.ring_first else 1
    scratch = room(8) + room(8) + room(SLOTS)
    scratch += room(ring_parts, 2) + room(ring_parts, 2) + room(ring_parts) + room(ring_parts)
    scratch += room(lambda p: 1 if p.ring_first else 4)
    scratch += room(3, 4)
    scratch += [pltpu.VMEM((p.rows, p.width // 4), p.dtype) for p in plans]
    scratch += [pltpu.VMEM((p.rows, p.width), p.dtype) for p in plans]
    copies = sum(8 + (9 if p.ring_first else 8) + 6 for p in plans)
    return pl.pallas_call(
        functools.partial(reduce_kernel, plans),
        out_shape=[jax.ShapeDtypeStruct((p.rows, p.width), jnp.float32) for p in plans],
        in_specs=[pl.BlockSpec(memory_space=pltpu.VMEM)] * (2 * len(plans)),
        out_specs=[pl.BlockSpec(memory_space=pltpu.VMEM)] * len(plans),
        scratch_shapes=scratch
        + [pltpu.SemaphoreType.DMA((copies,)), pltpu.SemaphoreType.DMA((copies,))],
        compiler_params=pltpu.CompilerParams(
            collective_id=1, has_side_effects=True, vmem_limit_bytes=62 * 1024 * 1024
        ),
    )(*lefts, *rights)


def relay_kernel(
    rows, cotangent, allowed, vec, bias_qkv, bias_up, hbm_qkv, hbm_out, hbm_up, hbm_down,
    section_out, section_grad, hidden_t, second_t, attended_t, normed_t, du, dbefore, db, dprojected, sums, sum_up,
    w_qkv, w_out, w_up, w_down, x, hat_one, scale_one, normed, qkv, probs, attended, middle, hat_two, scale_two,
    second, slope, hidden, wide, dmiddle, dattended, ship_out, ship_grad, land_out, land_grad, between,
    load_sem, send_sem, recv_sem,
):
    section = lax.axis_index("section")
    first = section == 0
    loads = [
        pltpu.make_async_copy(source, target, load_sem.at[k])
        for k, (source, target) in enumerate(
            ((hbm_qkv, w_qkv), (hbm_out, w_out), (hbm_up, w_up), (hbm_down, w_down))
        )
    ]
    for load in loads:
        load.start()
    shard = lax.axis_index("shard")
    height = section * 2 + shard // 8

    def beside(step):
        there = (height + step) % 4
        return {"section": there // 2, "shard": (there % 2) * 8 + shard % 8}

    barrier = pltpu.get_barrier_semaphore()
    for step in (1, 3):
        pl.semaphore_signal(barrier, inc=1, device_id=beside(step), device_id_type=MESH)
    pl.semaphore_wait(barrier, 2)

    def hop(source, land, which):
        begun = []

        def send(start, target, part, far, way):
            k = ((which * 2 + part) * 2 + far) * 2 + way
            copy = pltpu.make_async_remote_copy(
                src_ref=start, dst_ref=target, send_sem=send_sem.at[k], recv_sem=recv_sem.at[k],
                device_id=beside((1, 3)[way]), device_id_type=MESH,
            )
            copy.start()
            begun.append(copy)
            return copy

        def view(ref, part, way):
            return ref.at[pl.ds(way * SLOT, SLOT), pl.ds(part * 512, 512)]

        near, far = {}, {}

        def begin(part):
            for way in range(2):
                near[part, way] = send(view(source, part, way), view(between.at[which], part, way), part, 0, way)

        def end():
            for part in range(2):
                for way in range(2):
                    near[part, way].wait_recv()
                    far[part, way] = send(view(between.at[which], part, way), view(land, part, way), part, 1, way)
            for copy in far.values():
                copy.wait_recv()
            for copy in begun:
                copy.wait_send()

        return begin, end

    def tiles(width, body, tile=512):
        @pl.loop(0, width // tile)
        def _(step):
            body(pl.ds(pl.multiple_of(step * tile, 128), tile))

    ln1_gain, ln1_bias, _, _, b_out, ln2_gain, ln2_bias, b_down = (vec[k : k + 1, :] for k in range(8))
    low_half = lax.broadcasted_iota(jnp.int32, (SLOT, 128), 1) < 64

    def stacked(values):
        none = jnp.zeros_like(values)
        return jnp.concatenate([jnp.where(low_half, values, none), jnp.where(low_half, none, values)], axis=0)

    def unstacked(values):
        return jnp.where(low_half, values[:SLOT], values[SLOT:])

    def standard(values):
        centered = values - jnp.mean(values, axis=-1, keepdims=True)
        scale = lax.rsqrt(jnp.mean(centered * centered, axis=-1, keepdims=True) + norm_eps)
        return centered * scale, scale

    def forward(result, before_use, made=None):
        hat, scale = standard(x[...].astype(jnp.float32))
        hat_one[...] = hat
        scale_one[...] = scale
        normed[...] = (hat * ln1_gain + ln1_bias).astype(jnp.bfloat16)
        before_use(0)

        def project(cut):
            qkv[:, cut] = (dot(normed[...], w_qkv[:, cut]) + bias_qkv[:, cut]).astype(jnp.bfloat16)

        tiles(3072, project)

        @pl.loop(0, HEADS // 2)
        def _(couple):
            cuts = [pl.ds(pl.multiple_of(couple * 128 + 1024 * k, 128), 128) for k in range(3)]
            for slot in range(2):
                spot = pl.ds(slot * SLOT, SLOT)
                query, key, value = (qkv[spot, cut] for cut in cuts)
                scores = dot_back(stacked(query * SCALE), key)
                scores = jnp.where(allowed[slot] > 0, scores, masked_score)
                exponent = jnp.exp(scores - jnp.max(scores, axis=-1, keepdims=True))
                prob = exponent / jnp.sum(exponent, axis=-1, keepdims=True)
                probs[couple * 2 + slot] = prob
                mixed = dot(prob.astype(jnp.bfloat16), value)
                attended[spot, cuts[0]] = unstacked(mixed).astype(jnp.bfloat16)

        before_use(1)

        def mix(cut):
            branch = dot(attended[...], w_out[:, cut]) + vec[4:5, cut]
            middle[:, cut] = x[:, cut].astype(jnp.float32) + branch

        tiles(1024, mix)
        hat, scale = standard(middle[...])
        hat_two[...] = hat
        scale_two[...] = scale
        second[...] = (hat * ln2_gain + ln2_bias).astype(jnp.bfloat16)
        before_use(2)

        def grow(cut):
            before = dot(second[...], w_up[:, cut]) + bias_up[:, cut]
            square = before * before
            bend = jnp.tanh(GELU_A * (before + GELU_B * before * square))
            half = 0.5 * (1.0 + bend)
            hidden[:, cut] = (before * half).astype(jnp.bfloat16)
            slope[:, cut] = half + (0.5 * GELU_A) * before * (1.0 - bend * bend) * (1.0 + (3.0 * GELU_B) * square)

        tiles(4096, grow, 256)
        before_use(3)

        def shrink(cut):
            result[:, cut] = (middle[:, cut] + dot(hidden[...], w_down[:, cut]) + vec[7:8, cut]).astype(jnp.bfloat16)

        if made is None:
            tiles(1024, shrink)
        else:
            for part in range(2):
                shrink(pl.ds(part * 512, 512))
                made(part)

    def norm_back(hat, scale, grad, gain):
        inner = grad * gain
        return scale * (
            inner
            - jnp.mean(inner, axis=-1, keepdims=True)
            - hat * jnp.mean(inner * hat, axis=-1, keepdims=True)
        )

    def total(values):
        return jnp.sum(values.astype(jnp.float32), axis=0, keepdims=True)

    def backward(result, last):
        def grow_back(cut):
            grad = dot_back(du[...], w_down[cut, :]) * slope[:, cut]
            dbefore[:, cut] = grad.astype(jnp.bfloat16)
            if last:
                sum_up[:, cut] = total(dbefore[:, cut])

        tiles(4096, grow_back)

        def second_back(cut):
            wide[:, cut] = dot_back(dbefore[...], w_up[cut, :])

        tiles(1024, second_back)
        grad = wide[...]
        if last:
            sums[5:6, :] = jnp.sum(grad * hat_two[...], axis=0, keepdims=True)
            sums[6:7, :] = total(grad)
            sums[7:8, :] = total(du[...])
        dmiddle[...] = du[...].astype(jnp.float32) + norm_back(hat_two[...], scale_two[...], grad, ln2_gain)
        db[...] = dmiddle[...].astype(jnp.bfloat16)

        def mix_back(cut):
            dattended[:, cut] = dot_back(db[...], w_out[cut, :]).astype(jnp.bfloat16)

        tiles(1024, mix_back)

        @pl.loop(0, HEADS // 2)
        def _(couple):
            cuts = [pl.ds(pl.multiple_of(couple * 128 + 1024 * k, 128), 128) for k in range(3)]
            for slot in range(2):
                spot = pl.ds(slot * SLOT, SLOT)
                query, key, value = (qkv[spot, cut] for cut in cuts)
                grad = dattended[spot, cuts[0]]
                grads = stacked(grad)
                prob = probs[couple * 2 + slot]
                dprob = dot_back(grads, value)
                delta = jnp.sum(prob * dprob, axis=-1, keepdims=True)
                dscore = (prob * (dprob - delta)).astype(jnp.bfloat16)
                dprojected[spot, cuts[0]] = (unstacked(dot(dscore, key)) * 0.125).astype(jnp.bfloat16)
                dprojected[spot, cuts[1]] = dot_rows(dscore, stacked(query * SCALE)).astype(jnp.bfloat16)
                dprojected[spot, cuts[2]] = dot_rows(prob.astype(jnp.bfloat16), grads).astype(jnp.bfloat16)

        def normed_back(cut):
            wide[:, cut] = dot_back(dprojected[...], w_qkv[cut, :])

        tiles(1024, normed_back)
        grad = wide[...]
        result[...] = (dmiddle[...] + norm_back(hat_one[...], scale_one[...], grad, ln1_gain)).astype(jnp.bfloat16)
        if last:
            sums[0:1, :] = jnp.sum(grad * hat_one[...], axis=0, keepdims=True)
            sums[1:2, :] = total(grad)
            sums[2:3, :] = total(dprojected[:, :1024])
            sums[3:4, :] = total(dprojected[:, 2048:])
            sums[4:5, :] = total(db[...])

    x[...] = rows[...]
    begin, end = hop(ship_out, land_out, 0)
    forward(ship_out, lambda k: loads[k].wait(), begin)
    end()
    x[...] = jnp.where(first, rows[...], land_out[...])
    forward(section_out, lambda k: None)
    du[...] = cotangent[...]
    backward(ship_grad, False)
    begin, end = hop(ship_grad, land_grad, 1)
    begin(0)
    begin(1)

    def flip(source, target):
        def body(cut):
            target[cut, :] = source[:, cut].T

        tiles(source.shape[1], body, 256)

    for source, target in ((hidden, hidden_t), (second, second_t), (attended, attended_t), (normed, normed_t)):
        flip(source, target)
    end()
    du[...] = jnp.where(first, land_grad[...], cotangent[...])
    backward(section_grad, True)


def relay(rows, cotangent, allowed, vec, bias_qkv, bias_up, mats):
    tall, width, wide = rows.shape[0], rows.shape[1], mats[2].shape[1]
    low, full = jnp.bfloat16, jnp.float32
    outs = [
        ((tall, width), low), ((tall, width), low), ((wide, tall), low), ((width, tall), low), ((width, tall), low),
        ((width, tall), low), ((tall, width), low), ((tall, wide), low), ((tall, width), low),
        ((tall, 3 * width), low), ((8, width), full), ((1, wide), full),
    ]
    scratch = [(m.shape, low) for m in mats] + [
        ((tall, width), low), ((tall, width), full), ((tall, 1), full), ((tall, width), low),
        ((tall, 3 * width), low), ((HEADS, 2 * SLOT, SLOT), full), ((tall, width), low), ((tall, width), full),
        ((tall, width), full), ((tall, 1), full), ((tall, width), low), ((tall, wide), full), ((tall, wide), low),
        ((tall, width), full), ((tall, width), full), ((tall, width), low),
    ] + [((tall, width), low)] * 4 + [((2, tall, width), low)]
    in_vmem, anywhere = pl.BlockSpec(memory_space=pltpu.VMEM), pl.BlockSpec(memory_space=pl.ANY)
    return pl.pallas_call(
        relay_kernel,
        out_shape=[jax.ShapeDtypeStruct(*o) for o in outs],
        in_specs=[in_vmem] * 6 + [anywhere] * 4,
        out_specs=[in_vmem] * len(outs),
        scratch_shapes=[pltpu.VMEM(*s) for s in scratch]
        + [pltpu.SemaphoreType.DMA((n,)) for n in (4, 16, 16)],
        compiler_params=pltpu.CompilerParams(
            collective_id=2, has_side_effects=True, vmem_limit_bytes=62 * 1024 * 1024
        ),
    )(rows, cotangent, allowed, vec, bias_qkv, bias_up, *mats)


def allowed_pairs(segment):
    by_slot = segment.reshape(-1, SLOT)
    positions = jnp.arange(SLOT)
    allowed = (by_slot[:, :, None] == by_slot[:, None, :]) & (positions[None, :] <= positions[:, None])
    return jnp.concatenate([allowed, allowed], axis=1).astype(jnp.float32)


def on_device(
    ends, segment_ids, token_mask,
    ln1_gain, ln1_bias, w_qkv, b_query, b_value, w_out, b_out,
    ln2_gain, ln2_bias, w_up, b_up, w_down, b_down,
):
    width = ends.shape[2]
    shard_count = lax.axis_size("shard")
    packed = jnp.concatenate([ln1_gain, ln1_bias, b_query, b_value, b_out, ln2_gain, ln2_bias, b_down, b_up], axis=1)
    tall = jnp.broadcast_to(packed, (16, packed.shape[1]))
    *mats, everyone = gather_all((w_qkv[0], w_out[0], w_up[0], w_down[0], tall))
    everyone = everyone.reshape(shard_count, *tall.shape)[:, 0].astype(jnp.float32)
    piece = width // shard_count
    vec = everyone[:, : 8 * piece].reshape(shard_count, 8, piece).transpose(1, 0, 2).reshape(8, width)
    bias_up = everyone[:, 8 * piece :].reshape(1, -1)
    bias_qkv = jnp.concatenate([vec[2:3], jnp.zeros((1, width), jnp.float32), vec[3:4]], axis=1)

    local_rows = ends[0]
    cotangent = local_rows * token_mask[:, None].astype(jnp.bfloat16)
    (
        section_out, section_grad, hidden_t, second_t, attended_t, normed_t, du, dbefore, db, dprojected, sums, sum_up,
    ) = relay(local_rows, cotangent, allowed_pairs(segment_ids), vec, bias_qkv, bias_up, mats)

    rows = jnp.concatenate(
        [
            sums.reshape(8, shard_count, piece).transpose(1, 0, 2).reshape(shard_count, 8 * piece),
            sum_up.reshape(shard_count, -1),
        ],
        axis=1,
    )
    spread = jnp.pad(rows[:, None], ((0, 0), (0, 7), (0, 1024 - rows.shape[1])))
    g_down, g_up, g_out, g_qkv, mine = reduce_all(
        ((hidden_t, du), (second_t, dbefore), (attended_t, db), (normed_t, dprojected)), spread.reshape(-1, 1024)
    )
    out = [mine[:1, k * piece : (k + 1) * piece] for k in range(8)]
    g_ln1_gain, g_ln1_bias, g_query, g_value, g_b_out, g_ln2_gain, g_ln2_bias, g_b_down = out
    g_b_up = mine[:1, 8 * piece : 8 * piece + b_up.shape[1]]
    return (
        section_out[None], section_grad[None], g_ln1_gain, g_ln1_bias, g_qkv[None], g_query, g_value, g_out[None],
        g_b_out, g_ln2_gain, g_ln2_bias, g_up[None], g_b_up, g_down[None], g_b_down,
    )


def solution(mesh):
    vector, matrix = P("section", "shard"), P("section", "shard", None)
    rows, ids = P("section", ("dp", "shard"), None), P(("dp", "shard"))
    in_specs = (
        rows, ids, ids, vector, vector, matrix, vector, vector, matrix, vector, vector, vector, matrix,
        vector, matrix, vector,
    )
    out_specs = (
        rows, rows, vector, vector, matrix, vector, vector, matrix, vector, vector, vector, matrix, vector,
        matrix, vector,
    )
    return jax.shard_map(on_device, mesh=mesh, in_specs=in_specs, out_specs=out_specs, check_vma=False)
```

```python
import collections
import functools
import math

import jax
import jax.numpy as jnp
import numpy as np
from jax import lax
from jax.experimental import pallas as pl
from jax.experimental.pallas import tpu as pltpu
from jax.sharding import PartitionSpec as P

HEADS = 16
SLOT = 96
GELU_A = math.sqrt(2.0 / math.pi)
GELU_B = 0.044715

norm_eps = 1e-05
masked_score = -1e30
MESH = pl.DeviceIdType.MESH
SCALE = np.array(0.125, jnp.bfloat16)
RING_FIRST = (3,)
SPREAD = 2
FIRST_USED = (2, 4, 0, 1, 3)


def dot(left, right):
    return jnp.dot(left, right, preferred_element_type=jnp.float32)


def dot_rows(left, right):
    return lax.dot_general(
        left, right, (((0,), (0,)), ((), ())), preferred_element_type=jnp.float32
    )


def dot_back(left, right):
    return lax.dot_general(
        left, right, (((1,), (1,)), ((), ())), preferred_element_type=jnp.float32
    )


def gather_kernel(count, *refs):
    shards, fulls = refs[:count], refs[count : 2 * count]
    own_sem, send_sem, recv_sem = refs[2 * count :]
    me, plane = lax.axis_index("shard"), lax.axis_index("dp")
    core, x, y = me % 2, (me // 2) % 4, me // 8

    def at(dy, dx):
        return (((y + dy) % 2) * 4 + (x + dx) % 4) * 2 + core

    sibling = me + 1 - 2 * core
    right, left, pair = at(0, 1), at(0, 3), at(1, 0)
    barrier = pltpu.get_barrier_semaphore()
    neighbours = [{"shard": d} for d in (sibling, right, left, pair)]
    neighbours += [{"dp": (plane + k) % 4} for k in (1, 2, 3)]
    for other in neighbours:
        pl.semaphore_signal(barrier, inc=1, device_id=other, device_id_type=MESH)
    pl.semaphore_wait(barrier, len(neighbours))

    began = []

    def send(which, dy, dx, target, half=None, whole=False):
        rows, width = shards[which].shape
        mine = dy == 0 and dx == 0
        spot = pl.ds(pl.multiple_of(at(dy, dx) * rows, 16), rows)
        start = 0
        if which == SPREAD and not whole:
            width = width // 4
            start = pl.multiple_of(plane * width, 128)
        cut = pl.ds(start, width)
        if half is not None:
            cut = pl.ds(start + half * (width // 2), width // 2)
        source = shards[which].at[:, cut] if mine else fulls[which].at[spot, cut]
        copy = pltpu.make_async_remote_copy(
            src_ref=source,
            dst_ref=fulls[which].at[spot, cut],
            send_sem=send_sem.at[len(began)],
            recv_sem=recv_sem.at[len(began)],
            device_id=target if isinstance(target, dict) else {"shard": target},
            device_id_type=MESH,
        )
        copy.start()
        began.append(copy)
        return copy

    spreads = []

    def share(which, dy, dx):
        if which == SPREAD and (dy, dx) != (0, 0):
            copies = [send(which, dy, dx, {"dp": (plane + k) % 4}) for k in (2, 1, 3)]
            spreads.append((dy, dx, copies))
        else:
            shared.append(send(which, dy, dx, sibling, whole=True))

    pair_first = [k for k in FIRST_USED if k not in RING_FIRST]
    ring_first = [k for k in FIRST_USED if k in RING_FIRST]
    kept = []
    for k in range(count):
        rows = shards[k].shape[0]
        spot = pl.ds(pl.multiple_of(me * rows, 16), rows)
        copy = pltpu.make_async_copy(shards[k], fulls[k].at[spot, :], own_sem.at[k])
        copy.start()
        kept.append(copy)
    to_pair, to_right, to_left, shared = {}, {}, {}, []
    for k in pair_first:
        to_pair[k] = send(k, 0, 0, pair)
    for k in ring_first + pair_first:
        to_right[k] = send(k, 0, 0, right)
        to_left[k] = send(k, 0, 0, left)
    for k in ring_first:
        to_pair[k] = send(k, 0, 0, pair)
    for k in range(count):
        share(k, 0, 0)
    pair_right, pair_left = {}, {}
    for k in pair_first:
        to_pair[k].wait_recv()
        pair_right[k] = send(k, 1, 0, right)
        pair_left[k] = send(k, 1, 0, left)
        share(k, 1, 0)
    far, ring_pair = {}, {}
    for k in ring_first + pair_first:
        to_right[k].wait_recv()
        far[k, 0] = send(k, 0, 3, right, 0)
        if k in ring_first:
            ring_pair[k, 3] = send(k, 0, 3, pair)
        share(k, 0, 3)
        to_left[k].wait_recv()
        far[k, 1] = send(k, 0, 1, left, 1)
        if k in ring_first:
            ring_pair[k, 1] = send(k, 0, 1, pair)
        share(k, 0, 1)
    for k in ring_first:
        to_pair[k].wait_recv()
        share(k, 1, 0)
    for k in ring_first:
        far[k, 0].wait_recv()
        far[k, 1].wait_recv()
        ring_pair[k, 2] = send(k, 0, 2, pair)
        share(k, 0, 2)
    far_pair = {}
    for k in pair_first:
        pair_right[k].wait_recv()
        far_pair[k, 0] = send(k, 1, 3, right, 0)
        share(k, 1, 3)
        pair_left[k].wait_recv()
        far_pair[k, 1] = send(k, 1, 1, left, 1)
        share(k, 1, 1)
    for k in pair_first:
        far[k, 0].wait_recv()
        far[k, 1].wait_recv()
        share(k, 0, 2)
    for k in ring_first:
        for dx in (3, 1):
            ring_pair[k, dx].wait_recv()
            share(k, 1, dx)
    for k in pair_first:
        far_pair[k, 0].wait_recv()
        far_pair[k, 1].wait_recv()
        share(k, 1, 2)
    for k in ring_first:
        ring_pair[k, 2].wait_recv()
        share(k, 1, 2)
    for dy, dx, copies in spreads:
        for copy in copies:
            copy.wait_recv()
        shared.append(send(SPREAD, dy, dx, sibling, whole=True))
    for copy in shared:
        copy.wait_recv()
    for copy in began:
        copy.wait_send()
    for copy in kept:
        copy.wait()


def gather_all(arrays):
    count = len(arrays)
    copies = sum(16 if k in RING_FIRST else 17 for k in range(count)) + 21
    return pl.pallas_call(
        functools.partial(gather_kernel, count),
        out_shape=[jax.ShapeDtypeStruct((16 * a.shape[0], a.shape[1]), a.dtype) for a in arrays],
        in_specs=[pl.BlockSpec(memory_space=pl.ANY)] * count,
        out_specs=[pl.BlockSpec(memory_space=pl.ANY)] * count,
        scratch_shapes=[
            pltpu.SemaphoreType.DMA((count,)),
            pltpu.SemaphoreType.DMA((copies,)),
            pltpu.SemaphoreType.DMA((copies,)),
        ],
        compiler_params=pltpu.CompilerParams(collective_id=0, has_side_effects=True),
    )(*arrays)


def reduce_kernel(plans, *refs):
    count, given = len(plans), len({p.source for p in plans})
    refs = list(refs)

    def take(number):
        taken = refs[:number]
        del refs[:number]
        return taken

    lefts, rights = take(given), take(given)
    outs = take(given)
    lefts, rights = ([group[p.source] for p in plans] for group in (lefts, rights))
    sums, from_sibling, to_sibling = take(count), take(count), take(count)
    half_left, half_right, full_left, full_right, from_pair = (take(count) for _ in range(5))
    quarters, merged, spread = take(count), take(count), take(count)
    send_sem, recv_sem = refs

    me, plane = lax.axis_index("shard"), lax.axis_index("dp")
    core, x, y = me % 2, (me // 2) % 4, me // 8

    def chip(dy, dx):
        return ((y + dy) % 2) * 4 + (x + dx) % 4

    sibling = me + 1 - 2 * core
    right, left, pair = (chip(0, 1) * 2 + core, chip(0, 3) * 2 + core, chip(1, 0) * 2 + core)
    barrier = pltpu.get_barrier_semaphore()
    neighbours = [{"shard": d} for d in (sibling, right, left, pair)]
    neighbours += [{"dp": (plane + k) % 4} for k in (1, 2, 3)]
    for other in neighbours:
        pl.semaphore_signal(barrier, inc=1, device_id=other, device_id_type=MESH)
    pl.semaphore_wait(barrier, len(neighbours))

    began = []

    def send(source, target, device):
        copy = pltpu.make_async_remote_copy(
            src_ref=source,
            dst_ref=target,
            send_sem=send_sem.at[len(began)],
            recv_sem=recv_sem.at[len(began)],
            device_id=device,
            device_id_type=MESH,
        )
        copy.start()
        began.append(copy)
        return copy

    def tiles(width, body, tile=512):
        tile = min(tile, width) if width % tile == 0 or width < tile else 256

        @pl.loop(0, width // tile)
        def _(step):
            body(pl.ds(pl.multiple_of(step * tile, 128), tile))

    def add(where, *others):
        def body(cut):
            total = where[:, cut].astype(jnp.float32)
            for other in others:
                total = total + other[:, cut].astype(jnp.float32)
            where[:, cut] = total.astype(where.dtype)

        tiles(where.shape[1], body)

    width = [p.width for p in plans]
    lower = [pl.ds(0, w // 2) for w in width]
    upper = [pl.ds(w // 2, w // 2) for w in width]
    shared, waiting, slots = {}, [], [[] for _ in range(count)]
    halves, fulls, paired = {}, {}, {}

    def produce(k, dy, dx):
        rows, spot = plans[k].rows, dy * 4 + dx
        place = chip(dy, dx) * 2
        own = pl.ds(pl.multiple_of((place + core) * rows, rows), rows)
        others = pl.ds(pl.multiple_of((place + 1 - core) * rows, rows), rows)
        slot = len(slots[k]) % SLOTS
        if len(slots[k]) >= SLOTS:
            slots[k][-SLOTS].wait_send()
        if plans[k].product:
            both = jnp.concatenate([lefts[k][own, :], lefts[k][others, :]], axis=0)

            def body(cut):
                block = dot(both, rights[k][:, pl.ds(pl.multiple_of(plans[k].start + cut.start, 128), cut.size)])
                sums[k][spot, :, cut] = block[:rows].astype(sums[k].dtype)
                to_sibling[k][slot, :, cut] = block[rows:].astype(sums[k].dtype)

            tiles(width[k], body, 256 if rows > 64 else 512)
        else:
            sums[k][spot] = lefts[k][own, :]
            to_sibling[k][slot] = lefts[k][others, :]
        copy = send(to_sibling[k].at[slot], from_sibling[k].at[spot], {"shard": sibling})
        shared[k, dy, dx] = copy
        slots[k].append(copy)
        waiting.append((k, dy, dx))
        if len(waiting) > 2:
            settle(*waiting[0])

    def send_halves(k, dy):
        part = dy if plans[k].ring_first else 0
        halves[k, dy, 0] = send(
            sums[k].at[dy * 4 + 2, :, lower[k]], half_left[k].at[part], {"shard": right}
        )
        halves[k, dy, 1] = send(
            sums[k].at[dy * 4 + 2, :, upper[k]], half_right[k].at[part], {"shard": left}
        )

    def settle(k, dy, dx):
        if (k, dy, dx) not in waiting:
            return
        waiting.remove((k, dy, dx))
        spot = dy * 4 + dx
        shared[k, dy, dx].wait_recv()
        add(sums[k].at[spot], from_sibling[k].at[spot])
        if plans[k].ring_first:
            if dx == 2:
                send_halves(k, dy)
        elif dy == 1:
            paired[k, dx] = send(sums[k].at[spot], from_pair[k].at[dx], {"shard": pair})

    def forward(k, dy):
        part = dy if plans[k].ring_first else 0
        settle(k, dy, 1)
        halves[k, dy, 0].wait_recv()
        add(sums[k].at[dy * 4 + 1, :, lower[k]], half_left[k].at[part])
        fulls[k, dy, 0] = send(sums[k].at[dy * 4 + 1], full_left[k].at[part], {"shard": right})
        settle(k, dy, 3)
        halves[k, dy, 1].wait_recv()
        add(sums[k].at[dy * 4 + 3, :, upper[k]], half_right[k].at[part])
        fulls[k, dy, 1] = send(sums[k].at[dy * 4 + 3], full_right[k].at[part], {"shard": left})

    def meet(k, dx):
        settle(k, 0, dx)
        paired[k, dx].wait_recv()
        add(sums[k].at[dx], from_pair[k].at[dx])

    def ring_end(k, dy):
        part = dy if plans[k].ring_first else 0
        settle(k, dy, 0)
        fulls[k, dy, 0].wait_recv()
        fulls[k, dy, 1].wait_recv()
        add(sums[k].at[dy * 4], full_left[k].at[part], full_right[k].at[part])

    def cut_of(k, which):
        quarter = width[k] // 4
        return pl.ds(pl.multiple_of(which * quarter, 128), quarter)

    scattered, returned = {}, {}

    def scatter_planes(k):
        for hop in (2, 1, 3):
            there = (plane + hop) % 4
            scattered[k, hop] = send(sums[k].at[0, :, cut_of(k, there)], quarters[k].at[hop - 1], {"dp": there})

    def return_planes(k):
        for hop in (1, 2, 3):
            scattered[k, hop].wait_recv()
        total = sums[k][0, :, cut_of(k, plane)].astype(jnp.float32)
        for hop in range(3):
            total = total + quarters[k][hop].astype(jnp.float32)
        merged[k][...] = total.astype(merged[k].dtype)
        spread[k][:, cut_of(k, plane)] = merged[k][...]
        for hop in (2, 1, 3):
            there = (plane + hop) % 4
            returned[k, hop] = send(merged[k], spread[k].at[:, cut_of(k, plane)], {"dp": there})

    def finish(k):
        for hop in (1, 2, 3):
            returned[k, hop].wait_recv()

        result = outs[plans[k].source].at[:, pl.ds(plans[k].start, width[k])]

        def body(cut):
            result[:, cut] = spread[k][:, cut].astype(jnp.float32)

        tiles(width[k], body)

    def start_ring(k):
        produce(k, 1, 2)
        produce(k, 0, 2)

    def turn_ring(k):
        for dy in (1, 0):
            produce(k, dy, 1)
            produce(k, dy, 3)
            forward(k, dy)

    def to_pair(k):
        if plans[k].ring_first:
            produce(k, 1, 0)
            ring_end(k, 1)
            paired[k, 0] = send(sums[k].at[4], from_pair[k].at[0], {"shard": pair})
        else:
            for dx in (2, 1, 3, 0):
                produce(k, 1, dx)

    def late_start(k):
        produce(k, 0, 2)
        meet(k, 2)
        send_halves(k, 0)

    def late_turn(k):
        produce(k, 0, 1)
        produce(k, 0, 3)
        meet(k, 1)
        meet(k, 3)
        forward(k, 0)

    def conclude(k):
        produce(k, 0, 0)
        if plans[k].ring_first:
            ring_end(k, 0)
            paired[k, 0].wait_recv()
            add(sums[k].at[0], from_pair[k].at[0])
        else:
            meet(k, 0)
            ring_end(k, 0)
        scatter_planes(k)

    down_a, down_b, up_a, up_b, out, joint_a, joint_b, vectors = range(8)
    start_ring(up_a)
    produce(down_a, 1, 2)
    start_ring(up_b)
    for dx in (1, 3, 0):
        produce(down_a, 1, dx)
    turn_ring(up_a)
    start_ring(joint_a)
    to_pair(down_b)
    turn_ring(up_b)
    start_ring(vectors)
    late_start(down_a)
    to_pair(up_a)
    start_ring(joint_b)
    turn_ring(joint_a)
    to_pair(out)
    late_turn(down_a)
    to_pair(up_b)
    conclude(up_a)
    late_start(down_b)
    turn_ring(joint_b)
    turn_ring(vectors)
    to_pair(joint_a)
    conclude(down_a)
    conclude(up_b)
    return_planes(up_a)
    late_start(out)
    late_turn(down_b)
    to_pair(joint_b)
    to_pair(vectors)
    conclude(joint_a)
    return_planes(down_a)
    return_planes(up_b)
    late_turn(out)
    conclude(joint_b)
    conclude(vectors)
    return_planes(joint_a)
    conclude(down_b)
    return_planes(joint_b)
    return_planes(vectors)
    conclude(out)
    return_planes(down_b)
    return_planes(out)
    for k in (up_a, down_a, up_b, joint_a, joint_b, vectors, down_b, out):
        finish(k)
    kept_back = {id(c) for per in slots for c in per[:-SLOTS]}
    for copy in began:
        if id(copy) not in kept_back:
            copy.wait_send()


Plan = collections.namedtuple("Plan", ("source", "start", "rows", "width", "product", "ring_first", "dtype"))
SLOTS = 3


def reduce_all(pairs, vectors):
    plans = []
    for k, (left, right) in enumerate(pairs):
        parts = 1 if right.shape[1] == left.shape[0] else 2
        width = right.shape[1] // parts
        for part in range(parts):
            plans.append(Plan(k, part * width, left.shape[0] // 16, width, True, k in (1, 3), jnp.bfloat16))
    plans.append(Plan(len(pairs), 0, vectors.shape[0] // 16, vectors.shape[1], False, True, jnp.float32))
    lefts = [left for left, _ in pairs] + [vectors]
    rights = [right for _, right in pairs] + [jnp.zeros((8, 128), jnp.float32)]

    def room(depth, part=1):
        return [
            pltpu.VMEM((depth(p) if callable(depth) else depth, p.rows, p.width // part), p.dtype) for p in plans
        ]

    ring_parts = lambda p: 2 if p.ring_first else 1
    scratch = room(8) + room(8) + room(SLOTS)
    scratch += room(ring_parts, 2) + room(ring_parts, 2) + room(ring_parts) + room(ring_parts)
    scratch += room(lambda p: 1 if p.ring_first else 4)
    scratch += room(3, 4)
    scratch += [pltpu.VMEM((p.rows, p.width // 4), p.dtype) for p in plans]
    scratch += [pltpu.VMEM((p.rows, p.width), p.dtype) for p in plans]
    copies = sum(8 + (9 if p.ring_first else 8) + 6 for p in plans)
    return pl.pallas_call(
        functools.partial(reduce_kernel, plans),
        out_shape=[
            jax.ShapeDtypeStruct((left.shape[0] // 16, right.shape[1]), jnp.float32) for left, right in pairs
        ]
        + [jax.ShapeDtypeStruct((vectors.shape[0] // 16, vectors.shape[1]), jnp.float32)],
        in_specs=[pl.BlockSpec(memory_space=pltpu.VMEM)] * (2 * len(lefts)),
        out_specs=[pl.BlockSpec(memory_space=pltpu.VMEM)] * len(lefts),
        scratch_shapes=scratch
        + [pltpu.SemaphoreType.DMA((copies,)), pltpu.SemaphoreType.DMA((copies,))],
        compiler_params=pltpu.CompilerParams(
            collective_id=1, has_side_effects=True, vmem_limit_bytes=62 * 1024 * 1024
        ),
    )(*lefts, *rights)


def relay_kernel(
    rows, cotangent, allowed, vec, bias_qkv, bias_up, hbm_qkv, hbm_out, hbm_up, hbm_down,
    section_out, section_grad, hidden_t, second_t, attended_t, normed_t, du, dbefore, db, dprojected, sums, sum_up,
    w_qkv, w_out, w_up, w_down, x, hat_one, scale_one, normed, qkv, probs, attended, middle, hat_two, scale_two,
    second, slope, hidden, wide, dmiddle, dattended, ship_out, ship_grad, land_out, land_grad, between,
    load_sem, send_sem, recv_sem,
):
    section = lax.axis_index("section")
    first = section == 0
    loads = [
        pltpu.make_async_copy(source, target, load_sem.at[k])
        for k, (source, target) in enumerate(
            ((hbm_qkv, w_qkv), (hbm_out, w_out), (hbm_up, w_up), (hbm_down, w_down))
        )
    ]
    for load in loads:
        load.start()
    shard = lax.axis_index("shard")
    height = section * 2 + shard // 8

    def beside(step):
        there = (height + step) % 4
        return {"section": there // 2, "shard": (there % 2) * 8 + shard % 8}

    barrier = pltpu.get_barrier_semaphore()
    for step in (1, 3):
        pl.semaphore_signal(barrier, inc=1, device_id=beside(step), device_id_type=MESH)
    pl.semaphore_wait(barrier, 2)

    def hop(source, land, which):
        begun = []

        def send(start, target, part, far, way):
            k = ((which * 2 + part) * 2 + far) * 2 + way
            copy = pltpu.make_async_remote_copy(
                src_ref=start, dst_ref=target, send_sem=send_sem.at[k], recv_sem=recv_sem.at[k],
                device_id=beside((1, 3)[way]), device_id_type=MESH,
            )
            copy.start()
            begun.append(copy)
            return copy

        def view(ref, part, way):
            return ref.at[pl.ds(way * SLOT, SLOT), pl.ds(part * 512, 512)]

        near, far = {}, {}

        def begin(part):
            for way in range(2):
                near[part, way] = send(view(source, part, way), view(between.at[which], part, way), part, 0, way)

        def end():
            for part in range(2):
                for way in range(2):
                    near[part, way].wait_recv()
                    far[part, way] = send(view(between.at[which], part, way), view(land, part, way), part, 1, way)
            for copy in far.values():
                copy.wait_recv()
            for copy in begun:
                copy.wait_send()

        return begin, end

    def tiles(width, body, tile=512):
        @pl.loop(0, width // tile)
        def _(step):
            body(pl.ds(pl.multiple_of(step * tile, 128), tile))

    ln1_gain, ln1_bias, _, _, b_out, ln2_gain, ln2_bias, b_down = (vec[k : k + 1, :] for k in range(8))
    low_half = lax.broadcasted_iota(jnp.int32, (SLOT, 128), 1) < 64

    def stacked(values):
        none = jnp.zeros_like(values)
        return jnp.concatenate([jnp.where(low_half, values, none), jnp.where(low_half, none, values)], axis=0)

    def unstacked(values):
        return jnp.where(low_half, values[:SLOT], values[SLOT:])

    def standard(values):
        centered = values - jnp.mean(values, axis=-1, keepdims=True)
        scale = lax.rsqrt(jnp.mean(centered * centered, axis=-1, keepdims=True) + norm_eps)
        return centered * scale, scale

    def forward(result, before_use, made=None):
        hat, scale = standard(x[...].astype(jnp.float32))
        hat_one[...] = hat
        scale_one[...] = scale
        normed[...] = (hat * ln1_gain + ln1_bias).astype(jnp.bfloat16)
        before_use(0)

        def project(cut):
            qkv[:, cut] = (dot(normed[...], w_qkv[:, cut]) + bias_qkv[:, cut]).astype(jnp.bfloat16)

        tiles(3072, project)

        @pl.loop(0, HEADS // 2)
        def _(couple):
            cuts = [pl.ds(pl.multiple_of(couple * 128 + 1024 * k, 128), 128) for k in range(3)]
            for slot in range(2):
                spot = pl.ds(slot * SLOT, SLOT)
                query, key, value = (qkv[spot, cut] for cut in cuts)
                scores = dot_back(stacked(query * SCALE), key)
                scores = jnp.where(allowed[slot] > 0, scores, masked_score)
                exponent = jnp.exp(scores - jnp.max(scores, axis=-1, keepdims=True))
                prob = exponent / jnp.sum(exponent, axis=-1, keepdims=True)
                probs[couple * 2 + slot] = prob
                mixed = dot(prob.astype(jnp.bfloat16), value)
                attended[spot, cuts[0]] = unstacked(mixed).astype(jnp.bfloat16)

        before_use(1)

        def mix(cut):
            branch = dot(attended[...], w_out[:, cut]) + vec[4:5, cut]
            middle[:, cut] = x[:, cut].astype(jnp.float32) + branch

        tiles(1024, mix)
        hat, scale = standard(middle[...])
        hat_two[...] = hat
        scale_two[...] = scale
        second[...] = (hat * ln2_gain + ln2_bias).astype(jnp.bfloat16)
        before_use(2)

        def grow(cut):
            before = dot(second[...], w_up[:, cut]) + bias_up[:, cut]
            square = before * before
            bend = jnp.tanh(GELU_A * (before + GELU_B * before * square))
            half = 0.5 * (1.0 + bend)
            hidden[:, cut] = (before * half).astype(jnp.bfloat16)
            slope[:, cut] = half + (0.5 * GELU_A) * before * (1.0 - bend * bend) * (1.0 + (3.0 * GELU_B) * square)

        tiles(4096, grow, 256)
        before_use(3)

        def shrink(cut):
            result[:, cut] = (middle[:, cut] + dot(hidden[...], w_down[:, cut]) + vec[7:8, cut]).astype(jnp.bfloat16)

        if made is None:
            tiles(1024, shrink)
        else:
            for part in range(2):
                shrink(pl.ds(part * 512, 512))
                made(part)

    def norm_back(hat, scale, grad, gain):
        inner = grad * gain
        return scale * (
            inner
            - jnp.mean(inner, axis=-1, keepdims=True)
            - hat * jnp.mean(inner * hat, axis=-1, keepdims=True)
        )

    def total(values):
        return jnp.sum(values.astype(jnp.float32), axis=0, keepdims=True)

    def backward(result, last):
        def grow_back(cut):
            grad = dot_back(du[...], w_down[cut, :]) * slope[:, cut]
            dbefore[:, cut] = grad.astype(jnp.bfloat16)
            if last:
                sum_up[:, cut] = total(dbefore[:, cut])

        tiles(4096, grow_back)

        def second_back(cut):
            wide[:, cut] = dot_back(dbefore[...], w_up[cut, :])

        tiles(1024, second_back)
        grad = wide[...]
        if last:
            sums[5:6, :] = jnp.sum(grad * hat_two[...], axis=0, keepdims=True)
            sums[6:7, :] = total(grad)
            sums[7:8, :] = total(du[...])
        dmiddle[...] = du[...].astype(jnp.float32) + norm_back(hat_two[...], scale_two[...], grad, ln2_gain)
        db[...] = dmiddle[...].astype(jnp.bfloat16)

        def mix_back(cut):
            dattended[:, cut] = dot_back(db[...], w_out[cut, :]).astype(jnp.bfloat16)

        tiles(1024, mix_back)

        @pl.loop(0, HEADS // 2)
        def _(couple):
            cuts = [pl.ds(pl.multiple_of(couple * 128 + 1024 * k, 128), 128) for k in range(3)]
            for slot in range(2):
                spot = pl.ds(slot * SLOT, SLOT)
                query, key, value = (qkv[spot, cut] for cut in cuts)
                grad = dattended[spot, cuts[0]]
                grads = stacked(grad)
                prob = probs[couple * 2 + slot]
                dprob = dot_back(grads, value)
                delta = jnp.sum(prob * dprob, axis=-1, keepdims=True)
                dscore = (prob * (dprob - delta)).astype(jnp.bfloat16)
                dprojected[spot, cuts[0]] = (unstacked(dot(dscore, key)) * 0.125).astype(jnp.bfloat16)
                dprojected[spot, cuts[1]] = dot_rows(dscore, stacked(query * SCALE)).astype(jnp.bfloat16)
                dprojected[spot, cuts[2]] = dot_rows(prob.astype(jnp.bfloat16), grads).astype(jnp.bfloat16)

        def normed_back(cut):
            wide[:, cut] = dot_back(dprojected[...], w_qkv[cut, :])

        tiles(1024, normed_back)
        grad = wide[...]
        result[...] = (dmiddle[...] + norm_back(hat_one[...], scale_one[...], grad, ln1_gain)).astype(jnp.bfloat16)
        if last:
            sums[0:1, :] = jnp.sum(grad * hat_one[...], axis=0, keepdims=True)
            sums[1:2, :] = total(grad)
            sums[2:3, :] = total(dprojected[:, :1024])
            sums[3:4, :] = total(dprojected[:, 2048:])
            sums[4:5, :] = total(db[...])

    x[...] = rows[...]
    begin, end = hop(ship_out, land_out, 0)
    forward(ship_out, lambda k: loads[k].wait(), begin)
    end()
    x[...] = jnp.where(first, rows[...], land_out[...])
    forward(section_out, lambda k: None)
    du[...] = cotangent[...]
    backward(ship_grad, False)
    begin, end = hop(ship_grad, land_grad, 1)
    begin(0)
    begin(1)

    def flip(source, target):
        def body(cut):
            target[cut, :] = source[:, cut].T

        tiles(source.shape[1], body, 256)

    for source, target in ((hidden, hidden_t), (second, second_t), (attended, attended_t), (normed, normed_t)):
        flip(source, target)
    end()
    du[...] = jnp.where(first, land_grad[...], cotangent[...])
    backward(section_grad, True)


def relay(rows, cotangent, allowed, vec, bias_qkv, bias_up, mats):
    tall, width, wide = rows.shape[0], rows.shape[1], mats[2].shape[1]
    low, full = jnp.bfloat16, jnp.float32
    outs = [
        ((tall, width), low), ((tall, width), low), ((wide, tall), low), ((width, tall), low), ((width, tall), low),
        ((width, tall), low), ((tall, width), low), ((tall, wide), low), ((tall, width), low),
        ((tall, 3 * width), low), ((8, width), full), ((1, wide), full),
    ]
    scratch = [(m.shape, low) for m in mats] + [
        ((tall, width), low), ((tall, width), full), ((tall, 1), full), ((tall, width), low),
        ((tall, 3 * width), low), ((HEADS, 2 * SLOT, SLOT), full), ((tall, width), low), ((tall, width), full),
        ((tall, width), full), ((tall, 1), full), ((tall, width), low), ((tall, wide), full), ((tall, wide), low),
        ((tall, width), full), ((tall, width), full), ((tall, width), low),
    ] + [((tall, width), low)] * 4 + [((2, tall, width), low)]
    in_vmem, anywhere = pl.BlockSpec(memory_space=pltpu.VMEM), pl.BlockSpec(memory_space=pl.ANY)
    return pl.pallas_call(
        relay_kernel,
        out_shape=[jax.ShapeDtypeStruct(*o) for o in outs],
        in_specs=[in_vmem] * 6 + [anywhere] * 4,
        out_specs=[in_vmem] * len(outs),
        scratch_shapes=[pltpu.VMEM(*s) for s in scratch]
        + [pltpu.SemaphoreType.DMA((n,)) for n in (4, 16, 16)],
        compiler_params=pltpu.CompilerParams(
            collective_id=2, has_side_effects=True, vmem_limit_bytes=62 * 1024 * 1024
        ),
    )(rows, cotangent, allowed, vec, bias_qkv, bias_up, *mats)


def allowed_pairs(segment):
    by_slot = segment.reshape(-1, SLOT)
    positions = jnp.arange(SLOT)
    allowed = (by_slot[:, :, None] == by_slot[:, None, :]) & (positions[None, :] <= positions[:, None])
    return jnp.concatenate([allowed, allowed], axis=1).astype(jnp.float32)


def on_device(
    ends, segment_ids, token_mask,
    ln1_gain, ln1_bias, w_qkv, b_query, b_value, w_out, b_out,
    ln2_gain, ln2_bias, w_up, b_up, w_down, b_down,
):
    width = ends.shape[2]
    shard_count = lax.axis_size("shard")
    packed = jnp.concatenate([ln1_gain, ln1_bias, b_query, b_value, b_out, ln2_gain, ln2_bias, b_down, b_up], axis=1)
    tall = jnp.broadcast_to(packed, (16, packed.shape[1]))
    *mats, everyone = gather_all((w_qkv[0], w_out[0], w_up[0], w_down[0], tall))
    everyone = everyone.reshape(shard_count, *tall.shape)[:, 0].astype(jnp.float32)
    piece = width // shard_count
    vec = everyone[:, : 8 * piece].reshape(shard_count, 8, piece).transpose(1, 0, 2).reshape(8, width)
    bias_up = everyone[:, 8 * piece :].reshape(1, -1)
    bias_qkv = jnp.concatenate([vec[2:3], jnp.zeros((1, width), jnp.float32), vec[3:4]], axis=1)

    local_rows = ends[0]
    cotangent = local_rows * token_mask[:, None].astype(jnp.bfloat16)
    (
        section_out, section_grad, hidden_t, second_t, attended_t, normed_t, du, dbefore, db, dprojected, sums, sum_up,
    ) = relay(local_rows, cotangent, allowed_pairs(segment_ids), vec, bias_qkv, bias_up, mats)

    rows = jnp.concatenate(
        [
            sums.reshape(8, shard_count, piece).transpose(1, 0, 2).reshape(shard_count, 8 * piece),
            sum_up.reshape(shard_count, -1),
        ],
        axis=1,
    )
    spread = jnp.pad(rows[:, None], ((0, 0), (0, 7), (0, 1024 - rows.shape[1])))
    g_down, g_up, g_out, g_qkv, mine = reduce_all(
        ((hidden_t, du), (second_t, dbefore), (attended_t, db), (normed_t, dprojected)), spread.reshape(-1, 1024)
    )
    out = [mine[:1, k * piece : (k + 1) * piece] for k in range(8)]
    g_ln1_gain, g_ln1_bias, g_query, g_value, g_b_out, g_ln2_gain, g_ln2_bias, g_b_down = out
    g_b_up = mine[:1, 8 * piece : 8 * piece + b_up.shape[1]]
    return (
        section_out[None], section_grad[None], g_ln1_gain, g_ln1_bias, g_qkv[None], g_query, g_value, g_out[None],
        g_b_out, g_ln2_gain, g_ln2_bias, g_up[None], g_b_up, g_down[None], g_b_down,
    )


def solution(mesh):
    vector, matrix = P("section", "shard"), P("section", "shard", None)
    rows, ids = P("section", ("dp", "shard"), None), P(("dp", "shard"))
    in_specs = (
        rows, ids, ids, vector, vector, matrix, vector, vector, matrix, vector, vector, vector, matrix,
        vector, matrix, vector,
    )
    out_specs = (
        rows, rows, vector, vector, matrix, vector, vector, matrix, vector, vector, vector, matrix, vector,
        matrix, vector,
    )
    return jax.shard_map(on_device, mesh=mesh, in_specs=in_specs, out_specs=out_specs, check_vma=False)
```

```python
import collections
import functools
import math

import jax
import jax.numpy as jnp
import numpy as np
from jax import lax
from jax.experimental import pallas as pl
from jax.experimental.pallas import tpu as pltpu
from jax.sharding import PartitionSpec as P

HEADS = 16
SLOT = 96
GELU_A = math.sqrt(2.0 / math.pi)
GELU_B = 0.044715

norm_eps = 1e-05
masked_score = -1e30
MESH = pl.DeviceIdType.MESH
SCALE = np.array(0.125, jnp.bfloat16)
RING_FIRST = (3,)
SPREAD = 2
FIRST_USED = (2, 4, 0, 1, 3)


def dot(left, right):
    return jnp.dot(left, right, preferred_element_type=jnp.float32)


def dot_rows(left, right):
    return lax.dot_general(
        left, right, (((0,), (0,)), ((), ())), preferred_element_type=jnp.float32
    )


def dot_back(left, right):
    return lax.dot_general(
        left, right, (((1,), (1,)), ((), ())), preferred_element_type=jnp.float32
    )


def gather_kernel(count, *refs):
    shards, fulls = refs[:count], refs[count : 2 * count]
    own_sem, send_sem, recv_sem = refs[2 * count :]
    me, plane = lax.axis_index("shard"), lax.axis_index("dp")
    core, x, y = me % 2, (me // 2) % 4, me // 8

    def at(dy, dx):
        return (((y + dy) % 2) * 4 + (x + dx) % 4) * 2 + core

    sibling = me + 1 - 2 * core
    right, left, pair = at(0, 1), at(0, 3), at(1, 0)
    barrier = pltpu.get_barrier_semaphore()
    neighbours = [{"shard": d} for d in (sibling, right, left, pair)]
    neighbours += [{"dp": (plane + k) % 4} for k in (1, 2, 3)]
    for other in neighbours:
        pl.semaphore_signal(barrier, inc=1, device_id=other, device_id_type=MESH)
    pl.semaphore_wait(barrier, len(neighbours))

    began = []

    def send(which, dy, dx, target, half=None, whole=False):
        rows, width = shards[which].shape
        mine = dy == 0 and dx == 0
        spot = pl.ds(pl.multiple_of(at(dy, dx) * rows, 16), rows)
        start = 0
        if which == SPREAD and not whole:
            width = width // 4
            start = pl.multiple_of(plane * width, 128)
        cut = pl.ds(start, width)
        if half is not None:
            cut = pl.ds(start + half * (width // 2), width // 2)
        source = shards[which].at[:, cut] if mine else fulls[which].at[spot, cut]
        copy = pltpu.make_async_remote_copy(
            src_ref=source,
            dst_ref=fulls[which].at[spot, cut],
            send_sem=send_sem.at[len(began)],
            recv_sem=recv_sem.at[len(began)],
            device_id=target if isinstance(target, dict) else {"shard": target},
            device_id_type=MESH,
        )
        copy.start()
        began.append(copy)
        return copy

    spreads = []

    def share(which, dy, dx):
        if which == SPREAD and (dy, dx) != (0, 0):
            copies = [send(which, dy, dx, {"dp": (plane + k) % 4}) for k in (2, 1, 3)]
            spreads.append((dy, dx, copies))
        else:
            shared.append(send(which, dy, dx, sibling, whole=True))

    pair_first = [k for k in FIRST_USED if k not in RING_FIRST]
    ring_first = [k for k in FIRST_USED if k in RING_FIRST]
    kept = []
    for k in range(count):
        rows = shards[k].shape[0]
        spot = pl.ds(pl.multiple_of(me * rows, 16), rows)
        copy = pltpu.make_async_copy(shards[k], fulls[k].at[spot, :], own_sem.at[k])
        copy.start()
        kept.append(copy)
    to_pair, to_right, to_left, shared = {}, {}, {}, []
    for k in pair_first:
        to_pair[k] = send(k, 0, 0, pair)
    for k in ring_first + pair_first:
        to_right[k] = send(k, 0, 0, right)
        to_left[k] = send(k, 0, 0, left)
    for k in ring_first:
        to_pair[k] = send(k, 0, 0, pair)
    for k in range(count):
        share(k, 0, 0)
    pair_right, pair_left = {}, {}
    for k in pair_first:
        to_pair[k].wait_recv()
        pair_right[k] = send(k, 1, 0, right)
        pair_left[k] = send(k, 1, 0, left)
        share(k, 1, 0)
    far, ring_pair = {}, {}
    for k in ring_first + pair_first:
        to_right[k].wait_recv()
        far[k, 0] = send(k, 0, 3, right, 0)
        if k in ring_first:
            ring_pair[k, 3] = send(k, 0, 3, pair)
        share(k, 0, 3)
        to_left[k].wait_recv()
        far[k, 1] = send(k, 0, 1, left, 1)
        if k in ring_first:
            ring_pair[k, 1] = send(k, 0, 1, pair)
        share(k, 0, 1)
    for k in ring_first:
        to_pair[k].wait_recv()
        share(k, 1, 0)
    for k in ring_first:
        far[k, 0].wait_recv()
        far[k, 1].wait_recv()
        ring_pair[k, 2] = send(k, 0, 2, pair)
        share(k, 0, 2)
    far_pair = {}
    for k in pair_first:
        pair_right[k].wait_recv()
        far_pair[k, 0] = send(k, 1, 3, right, 0)
        share(k, 1, 3)
        pair_left[k].wait_recv()
        far_pair[k, 1] = send(k, 1, 1, left, 1)
        share(k, 1, 1)
    for k in pair_first:
        far[k, 0].wait_recv()
        far[k, 1].wait_recv()
        share(k, 0, 2)
    for k in ring_first:
        for dx in (3, 1):
            ring_pair[k, dx].wait_recv()
            share(k, 1, dx)
    for k in pair_first:
        far_pair[k, 0].wait_recv()
        far_pair[k, 1].wait_recv()
        share(k, 1, 2)
    for k in ring_first:
        ring_pair[k, 2].wait_recv()
        share(k, 1, 2)
    for dy, dx, copies in spreads:
        for copy in copies:
            copy.wait_recv()
        shared.append(send(SPREAD, dy, dx, sibling, whole=True))
    for copy in shared:
        copy.wait_recv()
    for copy in began:
        copy.wait_send()
    for copy in kept:
        copy.wait()


def gather_all(arrays):
    count = len(arrays)
    copies = sum(16 if k in RING_FIRST else 17 for k in range(count)) + 21
    return pl.pallas_call(
        functools.partial(gather_kernel, count),
        out_shape=[jax.ShapeDtypeStruct((16 * a.shape[0], a.shape[1]), a.dtype) for a in arrays],
        in_specs=[pl.BlockSpec(memory_space=pl.ANY)] * count,
        out_specs=[pl.BlockSpec(memory_space=pl.ANY)] * count,
        scratch_shapes=[
            pltpu.SemaphoreType.DMA((count,)),
            pltpu.SemaphoreType.DMA((copies,)),
            pltpu.SemaphoreType.DMA((copies,)),
        ],
        compiler_params=pltpu.CompilerParams(collective_id=0, has_side_effects=True),
    )(*arrays)


def reduce_kernel(plans, *refs):
    count, given = len(plans), len({p.source for p in plans})
    refs = list(refs)

    def take(number):
        taken = refs[:number]
        del refs[:number]
        return taken

    lefts, rights = take(given), take(given)
    outs = take(given)
    lefts, rights = ([group[p.source] for p in plans] for group in (lefts, rights))
    sums, from_sibling, to_sibling = take(count), take(count), take(count)
    half_left, half_right, full_left, full_right, from_pair = (take(count) for _ in range(5))
    quarters, merged, spread = take(count), take(count), take(count)
    send_sem, recv_sem = refs

    me, plane = lax.axis_index("shard"), lax.axis_index("dp")
    core, x, y = me % 2, (me // 2) % 4, me // 8

    def chip(dy, dx):
        return ((y + dy) % 2) * 4 + (x + dx) % 4

    sibling = me + 1 - 2 * core
    right, left, pair = (chip(0, 1) * 2 + core, chip(0, 3) * 2 + core, chip(1, 0) * 2 + core)
    barrier = pltpu.get_barrier_semaphore()
    neighbours = [{"shard": d} for d in (sibling, right, left, pair)]
    neighbours += [{"dp": (plane + k) % 4} for k in (1, 2, 3)]
    for other in neighbours:
        pl.semaphore_signal(barrier, inc=1, device_id=other, device_id_type=MESH)
    pl.semaphore_wait(barrier, len(neighbours))

    began = []

    def send(source, target, device):
        copy = pltpu.make_async_remote_copy(
            src_ref=source,
            dst_ref=target,
            send_sem=send_sem.at[len(began)],
            recv_sem=recv_sem.at[len(began)],
            device_id=device,
            device_id_type=MESH,
        )
        copy.start()
        began.append(copy)
        return copy

    def tiles(width, body, tile=512):
        tile = min(tile, width) if width % tile == 0 or width < tile else 256

        @pl.loop(0, width // tile)
        def _(step):
            body(pl.ds(pl.multiple_of(step * tile, 128), tile))

    def add(where, *others):
        def body(cut):
            total = where[:, cut].astype(jnp.float32)
            for other in others:
                total = total + other[:, cut].astype(jnp.float32)
            where[:, cut] = total.astype(where.dtype)

        tiles(where.shape[1], body)

    width = [p.width for p in plans]
    lower = [pl.ds(0, w // 2) for w in width]
    upper = [pl.ds(w // 2, w // 2) for w in width]
    shared, waiting, slots = {}, [], [[] for _ in range(count)]
    halves, fulls, paired = {}, {}, {}

    def produce(k, dy, dx):
        rows, spot = plans[k].rows, dy * 4 + dx
        place = chip(dy, dx) * 2
        own = pl.ds(pl.multiple_of((place + core) * rows, rows), rows)
        others = pl.ds(pl.multiple_of((place + 1 - core) * rows, rows), rows)
        slot = len(slots[k]) % SLOTS
        if len(slots[k]) >= SLOTS:
            slots[k][-SLOTS].wait_send()
        if plans[k].product:
            both = jnp.concatenate([lefts[k][own, :], lefts[k][others, :]], axis=0)

            def body(cut):
                block = dot(both, rights[k][:, pl.ds(pl.multiple_of(plans[k].start + cut.start, 128), cut.size)])
                sums[k][spot, :, cut] = block[:rows].astype(sums[k].dtype)
                to_sibling[k][slot, :, cut] = block[rows:].astype(sums[k].dtype)

            tiles(width[k], body, 256 if rows > 64 else 512)
        else:
            sums[k][spot] = lefts[k][own, :]
            to_sibling[k][slot] = lefts[k][others, :]
        copy = send(to_sibling[k].at[slot], from_sibling[k].at[spot], {"shard": sibling})
        shared[k, dy, dx] = copy
        slots[k].append(copy)
        waiting.append((k, dy, dx))
        if len(waiting) > 2:
            settle(*waiting[0])

    def send_halves(k, dy):
        part = dy if plans[k].ring_first else 0
        halves[k, dy, 0] = send(
            sums[k].at[dy * 4 + 2, :, lower[k]], half_left[k].at[part], {"shard": right}
        )
        halves[k, dy, 1] = send(
            sums[k].at[dy * 4 + 2, :, upper[k]], half_right[k].at[part], {"shard": left}
        )

    def settle(k, dy, dx):
        if (k, dy, dx) not in waiting:
            return
        waiting.remove((k, dy, dx))
        spot = dy * 4 + dx
        shared[k, dy, dx].wait_recv()
        add(sums[k].at[spot], from_sibling[k].at[spot])
        if plans[k].ring_first:
            if dx == 2:
                send_halves(k, dy)
        elif dy == 1:
            paired[k, dx] = send(sums[k].at[spot], from_pair[k].at[dx], {"shard": pair})

    def forward(k, dy):
        part = dy if plans[k].ring_first else 0
        settle(k, dy, 1)
        halves[k, dy, 0].wait_recv()
        add(sums[k].at[dy * 4 + 1, :, lower[k]], half_left[k].at[part])
        fulls[k, dy, 0] = send(sums[k].at[dy * 4 + 1], full_left[k].at[part], {"shard": right})
        settle(k, dy, 3)
        halves[k, dy, 1].wait_recv()
        add(sums[k].at[dy * 4 + 3, :, upper[k]], half_right[k].at[part])
        fulls[k, dy, 1] = send(sums[k].at[dy * 4 + 3], full_right[k].at[part], {"shard": left})

    def meet(k, dx):
        settle(k, 0, dx)
        paired[k, dx].wait_recv()
        add(sums[k].at[dx], from_pair[k].at[dx])

    def ring_end(k, dy):
        part = dy if plans[k].ring_first else 0
        settle(k, dy, 0)
        fulls[k, dy, 0].wait_recv()
        fulls[k, dy, 1].wait_recv()
        add(sums[k].at[dy * 4], full_left[k].at[part], full_right[k].at[part])

    def cut_of(k, which):
        quarter = width[k] // 4
        return pl.ds(pl.multiple_of(which * quarter, 128), quarter)

    scattered, returned = {}, {}

    def scatter_planes(k):
        for hop in (2, 1, 3):
            there = (plane + hop) % 4
            scattered[k, hop] = send(sums[k].at[0, :, cut_of(k, there)], quarters[k].at[hop - 1], {"dp": there})

    def return_planes(k):
        for hop in (1, 2, 3):
            scattered[k, hop].wait_recv()
        total = sums[k][0, :, cut_of(k, plane)].astype(jnp.float32)
        for hop in range(3):
            total = total + quarters[k][hop].astype(jnp.float32)
        merged[k][...] = total.astype(merged[k].dtype)
        spread[k][:, cut_of(k, plane)] = merged[k][...]
        for hop in (2, 1, 3):
            there = (plane + hop) % 4
            returned[k, hop] = send(merged[k], spread[k].at[:, cut_of(k, plane)], {"dp": there})

    def finish(k):
        for hop in (1, 2, 3):
            returned[k, hop].wait_recv()

        result = outs[plans[k].source].at[:, pl.ds(plans[k].start, width[k])]

        def body(cut):
            result[:, cut] = spread[k][:, cut].astype(jnp.float32)

        tiles(width[k], body)

    def start_ring(k):
        produce(k, 1, 2)
        produce(k, 0, 2)

    def turn_ring(k):
        for dy in (1, 0):
            produce(k, dy, 1)
            produce(k, dy, 3)
            forward(k, dy)

    def to_pair(k):
        if plans[k].ring_first:
            produce(k, 1, 0)
            ring_end(k, 1)
            paired[k, 0] = send(sums[k].at[4], from_pair[k].at[0], {"shard": pair})
        else:
            for dx in (2, 1, 3, 0):
                produce(k, 1, dx)

    def late_start(k):
        produce(k, 0, 2)
        meet(k, 2)
        send_halves(k, 0)

    def late_turn(k):
        produce(k, 0, 1)
        produce(k, 0, 3)
        meet(k, 1)
        meet(k, 3)
        forward(k, 0)

    def conclude(k):
        produce(k, 0, 0)
        if plans[k].ring_first:
            ring_end(k, 0)
            paired[k, 0].wait_recv()
            add(sums[k].at[0], from_pair[k].at[0])
        else:
            meet(k, 0)
            ring_end(k, 0)
        scatter_planes(k)

    down_a, down_b, up_a, up_b, out, joint_a, joint_b, vectors = range(8)
    start_ring(up_a)
    produce(down_a, 1, 2)
    start_ring(up_b)
    for dx in (1, 3, 0):
        produce(down_a, 1, dx)
    turn_ring(up_a)
    start_ring(joint_a)
    to_pair(down_b)
    turn_ring(up_b)
    start_ring(vectors)
    late_start(down_a)
    to_pair(up_a)
    start_ring(joint_b)
    turn_ring(joint_a)
    to_pair(out)
    late_turn(down_a)
    to_pair(up_b)
    conclude(up_a)
    late_start(down_b)
    turn_ring(joint_b)
    turn_ring(vectors)
    to_pair(joint_a)
    conclude(down_a)
    conclude(up_b)
    return_planes(up_a)
    late_start(out)
    late_turn(down_b)
    to_pair(joint_b)
    to_pair(vectors)
    conclude(joint_a)
    return_planes(down_a)
    return_planes(up_b)
    late_turn(out)
    conclude(joint_b)
    conclude(vectors)
    return_planes(joint_a)
    conclude(down_b)
    return_planes(joint_b)
    return_planes(vectors)
    conclude(out)
    return_planes(down_b)
    return_planes(out)
    for k in (up_a, down_a, up_b, joint_a, joint_b, vectors, down_b, out):
        finish(k)
    kept_back = {id(c) for per in slots for c in per[:-SLOTS]}
    for copy in began:
        if id(copy) not in kept_back:
            copy.wait_send()


Plan = collections.namedtuple("Plan", ("source", "start", "rows", "width", "product", "ring_first", "dtype"))
SLOTS = 3


def reduce_all(pairs, vectors):
    plans = []
    for k, (left, right) in enumerate(pairs):
        parts = 1 if right.shape[1] == left.shape[0] else 2
        width = right.shape[1] // parts
        for part in range(parts):
            plans.append(Plan(k, part * width, left.shape[0] // 16, width, True, k in (1, 3), jnp.bfloat16))
    plans.append(Plan(len(pairs), 0, vectors.shape[0] // 16, vectors.shape[1], False, True, jnp.float32))
    lefts = [left for left, _ in pairs] + [vectors]
    rights = [right for _, right in pairs] + [jnp.zeros((8, 128), jnp.float32)]

    def room(depth, part=1):
        return [
            pltpu.VMEM((depth(p) if callable(depth) else depth, p.rows, p.width // part), p.dtype) for p in plans
        ]

    ring_parts = lambda p: 2 if p.ring_first else 1
    scratch = room(8) + room(8) + room(SLOTS)
    scratch += room(ring_parts, 2) + room(ring_parts, 2) + room(ring_parts) + room(ring_parts)
    scratch += room(lambda p: 1 if p.ring_first else 4)
    scratch += room(3, 4)
    scratch += [pltpu.VMEM((p.rows, p.width // 4), p.dtype) for p in plans]
    scratch += [pltpu.VMEM((p.rows, p.width), p.dtype) for p in plans]
    copies = sum(8 + (9 if p.ring_first else 8) + 6 for p in plans)
    return pl.pallas_call(
        functools.partial(reduce_kernel, plans),
        out_shape=[
            jax.ShapeDtypeStruct((left.shape[0] // 16, right.shape[1]), jnp.float32) for left, right in pairs
        ]
        + [jax.ShapeDtypeStruct((vectors.shape[0] // 16, vectors.shape[1]), jnp.float32)],
        in_specs=[pl.BlockSpec(memory_space=pltpu.VMEM)] * (2 * len(lefts)),
        out_specs=[pl.BlockSpec(memory_space=pltpu.VMEM)] * len(lefts),
        scratch_shapes=scratch
        + [pltpu.SemaphoreType.DMA((copies,)), pltpu.SemaphoreType.DMA((copies,))],
        compiler_params=pltpu.CompilerParams(
            collective_id=1, has_side_effects=True, vmem_limit_bytes=62 * 1024 * 1024
        ),
    )(*lefts, *rights)


def relay_kernel(
    rows, cotangent, allowed, vec, bias_qkv, bias_up, hbm_qkv, hbm_out, hbm_up, hbm_down,
    section_out, section_grad, hidden_t, second_t, attended_t, normed_t, du, dbefore, db, dprojected, sums, sum_up,
    w_qkv, w_out, w_up, w_down, x, hat_one, scale_one, normed, qkv, probs, attended, middle, hat_two, scale_two,
    second, slope, hidden, wide, dmiddle, dattended, ship_out, ship_grad, land_out, land_grad, between,
    load_sem, send_sem, recv_sem,
):
    section = lax.axis_index("section")
    first = section == 0
    loads = [
        pltpu.make_async_copy(source, target, load_sem.at[k])
        for k, (source, target) in enumerate(
            ((hbm_qkv, w_qkv), (hbm_out, w_out), (hbm_up, w_up), (hbm_down, w_down))
        )
    ]
    for load in loads:
        load.start()
    shard = lax.axis_index("shard")
    height = section * 2 + shard // 8

    def beside(step):
        there = (height + step) % 4
        return {"section": there // 2, "shard": (there % 2) * 8 + shard % 8}

    barrier = pltpu.get_barrier_semaphore()
    for step in (1, 3):
        pl.semaphore_signal(barrier, inc=1, device_id=beside(step), device_id_type=MESH)
    pl.semaphore_wait(barrier, 2)

    def hop(source, land, which):
        begun = []

        def send(start, target, part, far, way):
            k = ((which * 2 + part) * 2 + far) * 2 + way
            copy = pltpu.make_async_remote_copy(
                src_ref=start, dst_ref=target, send_sem=send_sem.at[k], recv_sem=recv_sem.at[k],
                device_id=beside((1, 3)[way]), device_id_type=MESH,
            )
            copy.start()
            begun.append(copy)
            return copy

        def view(ref, part, way):
            return ref.at[pl.ds(way * SLOT, SLOT), pl.ds(part * 512, 512)]

        near, far = {}, {}

        def begin(part):
            for way in range(2):
                near[part, way] = send(view(source, part, way), view(between.at[which], part, way), part, 0, way)

        def end():
            for part in range(2):
                for way in range(2):
                    near[part, way].wait_recv()
                    far[part, way] = send(view(between.at[which], part, way), view(land, part, way), part, 1, way)
            for copy in far.values():
                copy.wait_recv()
            for copy in begun:
                copy.wait_send()

        return begin, end

    def tiles(width, body, tile=512):
        @pl.loop(0, width // tile)
        def _(step):
            body(pl.ds(pl.multiple_of(step * tile, 128), tile))

    ln1_gain, ln1_bias, _, _, b_out, ln2_gain, ln2_bias, b_down = (vec[k : k + 1, :] for k in range(8))
    low_half = lax.broadcasted_iota(jnp.int32, (SLOT, 128), 1) < 64

    def stacked(values):
        none = jnp.zeros_like(values)
        return jnp.concatenate([jnp.where(low_half, values, none), jnp.where(low_half, none, values)], axis=0)

    def unstacked(values):
        return jnp.where(low_half, values[:SLOT], values[SLOT:])

    def standard(values):
        centered = values - jnp.mean(values, axis=-1, keepdims=True)
        scale = lax.rsqrt(jnp.mean(centered * centered, axis=-1, keepdims=True) + norm_eps)
        return centered * scale, scale

    def forward(result, before_use, made=None):
        hat, scale = standard(x[...].astype(jnp.float32))
        hat_one[...] = hat
        scale_one[...] = scale
        normed[...] = (hat * ln1_gain + ln1_bias).astype(jnp.bfloat16)
        before_use(0)

        def project(cut):
            qkv[:, cut] = (dot(normed[...], w_qkv[:, cut]) + bias_qkv[:, cut]).astype(jnp.bfloat16)

        tiles(3072, project)

        @pl.loop(0, HEADS // 2, unroll=4)
        def _(couple):
            cuts = [pl.ds(pl.multiple_of(couple * 128 + 1024 * k, 128), 128) for k in range(3)]
            for slot in range(2):
                spot = pl.ds(slot * SLOT, SLOT)
                query, key, value = (qkv[spot, cut] for cut in cuts)
                scores = dot_back(stacked(query * SCALE), key)
                scores = jnp.where(allowed[slot] > 0, scores, masked_score)
                exponent = jnp.exp(scores - jnp.max(scores, axis=-1, keepdims=True))
                prob = exponent / jnp.sum(exponent, axis=-1, keepdims=True)
                probs[couple * 2 + slot] = prob
                mixed = dot(prob.astype(jnp.bfloat16), value)
                attended[spot, cuts[0]] = unstacked(mixed).astype(jnp.bfloat16)

        before_use(1)

        def mix(cut):
            branch = dot(attended[...], w_out[:, cut]) + vec[4:5, cut]
            middle[:, cut] = x[:, cut].astype(jnp.float32) + branch

        tiles(1024, mix)
        hat, scale = standard(middle[...])
        hat_two[...] = hat
        scale_two[...] = scale
        second[...] = (hat * ln2_gain + ln2_bias).astype(jnp.bfloat16)
        before_use(2)

        def grow(cut):
            before = dot(second[...], w_up[:, cut]) + bias_up[:, cut]
            square = before * before
            bend = jnp.tanh(GELU_A * (before + GELU_B * before * square))
            half = 0.5 * (1.0 + bend)
            hidden[:, cut] = (before * half).astype(jnp.bfloat16)
            slope[:, cut] = half + (0.5 * GELU_A) * before * (1.0 - bend * bend) * (1.0 + (3.0 * GELU_B) * square)

        tiles(4096, grow, 512)
        before_use(3)

        def shrink(cut):
            result[:, cut] = (middle[:, cut] + dot(hidden[...], w_down[:, cut]) + vec[7:8, cut]).astype(jnp.bfloat16)

        if made is None:
            tiles(1024, shrink)
        else:
            for part in range(2):
                shrink(pl.ds(part * 512, 512))
                made(part)

    def norm_back(hat, scale, grad, gain):
        inner = grad * gain
        return scale * (
            inner
            - jnp.mean(inner, axis=-1, keepdims=True)
            - hat * jnp.mean(inner * hat, axis=-1, keepdims=True)
        )

    def total(values):
        return jnp.sum(values.astype(jnp.float32), axis=0, keepdims=True)

    def backward(result, last):
        def grow_back(cut):
            grad = dot_back(du[...], w_down[cut, :]) * slope[:, cut]
            dbefore[:, cut] = grad.astype(jnp.bfloat16)
            if last:
                sum_up[:, cut] = total(dbefore[:, cut])

        tiles(4096, grow_back)

        def second_back(cut):
            wide[:, cut] = dot_back(dbefore[...], w_up[cut, :])

        tiles(1024, second_back)
        grad = wide[...]
        if last:
            sums[5:6, :] = jnp.sum(grad * hat_two[...], axis=0, keepdims=True)
            sums[6:7, :] = total(grad)
            sums[7:8, :] = total(du[...])
        dmiddle[...] = du[...].astype(jnp.float32) + norm_back(hat_two[...], scale_two[...], grad, ln2_gain)
        db[...] = dmiddle[...].astype(jnp.bfloat16)

        def mix_back(cut):
            dattended[:, cut] = dot_back(db[...], w_out[cut, :]).astype(jnp.bfloat16)

        tiles(1024, mix_back)

        @pl.loop(0, HEADS // 2, unroll=4)
        def _(couple):
            cuts = [pl.ds(pl.multiple_of(couple * 128 + 1024 * k, 128), 128) for k in range(3)]
            for slot in range(2):
                spot = pl.ds(slot * SLOT, SLOT)
                query, key, value = (qkv[spot, cut] for cut in cuts)
                grad = dattended[spot, cuts[0]]
                grads = stacked(grad)
                prob = probs[couple * 2 + slot]
                dprob = dot_back(grads, value)
                delta = jnp.sum(prob * dprob, axis=-1, keepdims=True)
                dscore = (prob * (dprob - delta)).astype(jnp.bfloat16)
                dprojected[spot, cuts[0]] = (unstacked(dot(dscore, key)) * 0.125).astype(jnp.bfloat16)
                dprojected[spot, cuts[1]] = dot_rows(dscore, stacked(query * SCALE)).astype(jnp.bfloat16)
                dprojected[spot, cuts[2]] = dot_rows(prob.astype(jnp.bfloat16), grads).astype(jnp.bfloat16)

        def normed_back(cut):
            wide[:, cut] = dot_back(dprojected[...], w_qkv[cut, :])

        tiles(1024, normed_back)
        grad = wide[...]
        result[...] = (dmiddle[...] + norm_back(hat_one[...], scale_one[...], grad, ln1_gain)).astype(jnp.bfloat16)
        if last:
            sums[0:1, :] = jnp.sum(grad * hat_one[...], axis=0, keepdims=True)
            sums[1:2, :] = total(grad)
            sums[2:3, :] = total(dprojected[:, :1024])
            sums[3:4, :] = total(dprojected[:, 2048:])
            sums[4:5, :] = total(db[...])

    x[...] = rows[...]
    begin, end = hop(ship_out, land_out, 0)
    forward(ship_out, lambda k: loads[k].wait(), begin)
    end()
    x[...] = jnp.where(first, rows[...], land_out[...])
    forward(section_out, lambda k: None)
    du[...] = cotangent[...]
    backward(ship_grad, False)
    begin, end = hop(ship_grad, land_grad, 1)
    begin(0)
    begin(1)

    def flip(source, target):
        def body(cut):
            target[cut, :] = source[:, cut].T

        tiles(source.shape[1], body, 256)

    for source, target in ((hidden, hidden_t), (second, second_t), (attended, attended_t), (normed, normed_t)):
        flip(source, target)
    end()
    du[...] = jnp.where(first, land_grad[...], cotangent[...])
    backward(section_grad, True)


def relay(rows, cotangent, allowed, vec, bias_qkv, bias_up, mats):
    tall, width, wide = rows.shape[0], rows.shape[1], mats[2].shape[1]
    low, full = jnp.bfloat16, jnp.float32
    outs = [
        ((tall, width), low), ((tall, width), low), ((wide, tall), low), ((width, tall), low), ((width, tall), low),
        ((width, tall), low), ((tall, width), low), ((tall, wide), low), ((tall, width), low),
        ((tall, 3 * width), low), ((8, width), full), ((1, wide), full),
    ]
    scratch = [(m.shape, low) for m in mats] + [
        ((tall, width), low), ((tall, width), full), ((tall, 1), full), ((tall, width), low),
        ((tall, 3 * width), low), ((HEADS, 2 * SLOT, SLOT), full), ((tall, width), low), ((tall, width), full),
        ((tall, width), full), ((tall, 1), full), ((tall, width), low), ((tall, wide), full), ((tall, wide), low),
        ((tall, width), full), ((tall, width), full), ((tall, width), low),
    ] + [((tall, width), low)] * 4 + [((2, tall, width), low)]
    in_vmem, anywhere = pl.BlockSpec(memory_space=pltpu.VMEM), pl.BlockSpec(memory_space=pl.ANY)
    return pl.pallas_call(
        relay_kernel,
        out_shape=[jax.ShapeDtypeStruct(*o) for o in outs],
        in_specs=[in_vmem] * 6 + [anywhere] * 4,
        out_specs=[in_vmem] * len(outs),
        scratch_shapes=[pltpu.VMEM(*s) for s in scratch]
        + [pltpu.SemaphoreType.DMA((n,)) for n in (4, 16, 16)],
        compiler_params=pltpu.CompilerParams(
            collective_id=2, has_side_effects=True, vmem_limit_bytes=62 * 1024 * 1024
        ),
    )(rows, cotangent, allowed, vec, bias_qkv, bias_up, *mats)


def allowed_pairs(segment):
    by_slot = segment.reshape(-1, SLOT)
    positions = jnp.arange(SLOT)
    allowed = (by_slot[:, :, None] == by_slot[:, None, :]) & (positions[None, :] <= positions[:, None])
    return jnp.concatenate([allowed, allowed], axis=1).astype(jnp.float32)


def on_device(
    ends, segment_ids, token_mask,
    ln1_gain, ln1_bias, w_qkv, b_query, b_value, w_out, b_out,
    ln2_gain, ln2_bias, w_up, b_up, w_down, b_down,
):
    width = ends.shape[2]
    shard_count = lax.axis_size("shard")
    packed = jnp.concatenate([ln1_gain, ln1_bias, b_query, b_value, b_out, ln2_gain, ln2_bias, b_down, b_up], axis=1)
    tall = jnp.broadcast_to(packed, (16, packed.shape[1]))
    *mats, everyone = gather_all((w_qkv[0], w_out[0], w_up[0], w_down[0], tall))
    everyone = everyone.reshape(shard_count, *tall.shape)[:, 0].astype(jnp.float32)
    piece = width // shard_count
    vec = everyone[:, : 8 * piece].reshape(shard_count, 8, piece).transpose(1, 0, 2).reshape(8, width)
    bias_up = everyone[:, 8 * piece :].reshape(1, -1)
    bias_qkv = jnp.concatenate([vec[2:3], jnp.zeros((1, width), jnp.float32), vec[3:4]], axis=1)

    local_rows = ends[0]
    cotangent = local_rows * token_mask[:, None].astype(jnp.bfloat16)
    (
        section_out, section_grad, hidden_t, second_t, attended_t, normed_t, du, dbefore, db, dprojected, sums, sum_up,
    ) = relay(local_rows, cotangent, allowed_pairs(segment_ids), vec, bias_qkv, bias_up, mats)

    rows = jnp.concatenate(
        [
            sums.reshape(8, shard_count, piece).transpose(1, 0, 2).reshape(shard_count, 8 * piece),
            sum_up.reshape(shard_count, -1),
        ],
        axis=1,
    )
    spread = jnp.pad(rows[:, None], ((0, 0), (0, 7), (0, 1024 - rows.shape[1])))
    g_down, g_up, g_out, g_qkv, mine = reduce_all(
        ((hidden_t, du), (second_t, dbefore), (attended_t, db), (normed_t, dprojected)), spread.reshape(-1, 1024)
    )
    out = [mine[:1, k * piece : (k + 1) * piece] for k in range(8)]
    g_ln1_gain, g_ln1_bias, g_query, g_value, g_b_out, g_ln2_gain, g_ln2_bias, g_b_down = out
    g_b_up = mine[:1, 8 * piece : 8 * piece + b_up.shape[1]]
    return (
        section_out[None], section_grad[None], g_ln1_gain, g_ln1_bias, g_qkv[None], g_query, g_value, g_out[None],
        g_b_out, g_ln2_gain, g_ln2_bias, g_up[None], g_b_up, g_down[None], g_b_down,
    )


def solution(mesh):
    vector, matrix = P("section", "shard"), P("section", "shard", None)
    rows, ids = P("section", ("dp", "shard"), None), P(("dp", "shard"))
    in_specs = (
        rows, ids, ids, vector, vector, matrix, vector, vector, matrix, vector, vector, vector, matrix,
        vector, matrix, vector,
    )
    out_specs = (
        rows, rows, vector, vector, matrix, vector, vector, matrix, vector, vector, vector, matrix, vector,
        matrix, vector,
    )
    return jax.shard_map(on_device, mesh=mesh, in_specs=in_specs, out_specs=out_specs, check_vma=False)
```
